128 devices in a mesh: ep: 32 (over y, z, core), tp: 4 (over x).
Axes of the slice: x: 4, y: 4, z: 4, core: 2. Of those that a mesh axis runs over, the one named last changes fastest.
Arguments:
- queries: bfloat16 [256, 64, 128], P('ep', 'tp'), may hold values from -115 to 115
- key_cache: bfloat16 [256, 4, 1024, 128], P('ep', 'tp'), may hold values from -6 to 6
- stored_value_cache: bfloat16 [256, 4, 1024, 128], P('ep', 'tp'), may hold values from -6 to 6
- new_key: bfloat16 [256, 4, 128], P('ep', 'tp'), may hold values from -4.5 to 4.5
- incoming_value: bfloat16 [256, 4, 128], P('ep', 'tp'), may hold values from -6 to 6
- lengths: int32 [256], P('ep'), may hold values from 1 to 1024, as said below
- policy: int32 [256, 4], P('ep', 'tp'), may hold values from 0 to 2
- retained_blocks: int32 [256, 4, 4], P('ep', 'tp'), may hold values from 0 to 15
- out_weight: bfloat16 [8192, 4096], P(None, 'ep'), may hold values from -0.5 to 0.5
- residual: bfloat16 [256, 4096], P(None, 'ep'), may hold values from -6 to 6
- norm_gain: float32 [4096], replicated, may hold values from 0.1 to 1.9
- routes: int32 [256, 8], replicated, may hold values from 0 to 63, all different within a row; in each aligned block of 256 rows (0 to 255, 256 to 511, ...) at most 64 rows name the same one
- router_logits: float32 [256, 8], replicated, may hold values from -6 to 6
- gate_weight: bfloat16 [64, 4096, 1536], P('ep', None, 'tp'), may hold values from -0.09375 to 0.09375
- up_weight: bfloat16 [64, 4096, 1536], P('ep', None, 'tp'), may hold values from -0.09375 to 0.09375
- down_weight: bfloat16 [64, 1536, 4096], P('ep', 'tp'), may hold values from -0.15625 to 0.15625
Outputs:
- mixed_out: bfloat16 [256, 4096], P(None, ('ep', 'tp'))
The draws below stay inside these ranges and needn't reach their ends.
Inputs may be any that keep to these rules, and one draw needn't show every extreme that they name: `lengths`: each aligned group of 8 requests holds one of length 1024. At most 64 of all routes name one expert, a bound that some block reaches; a token names 8 different experts.
All inputs are finite; a program needn't handle non-finite values.
Results may differ from the reference program's by a relative error of at most 0.015.
Values may be sent and summed in bfloat16 or wider, within the bound.
A program may use at most 128 MiB of HBM per device.

```python
import math
import jax
import jax.numpy as jnp
import numpy as np
from jax import lax

D = 4096
QUERY_HEADS = 64
KEY_VALUE_HEADS = 4
HEAD_DIMENSION = 128
FF = 1536
TOPK = 8
REQ_DEV = 8
BLK = 64
BLOCK_COUNT = 16
KEPT_ENTRIES = 4
WIN = 2
EXPERTS = 64
REQUEST_TOTAL = 256
CONTEXT_SLOTS = 1024
CAP = 64


def request_lengths(key):
    sampled_values = jax.random.randint(jax.random.fold_in(key, 11), (REQUEST_TOTAL,), 1, CONTEXT_SLOTS + 1, dtype=jnp.int32)
    groups = REQUEST_TOTAL // REQ_DEV
    full_slot = jax.random.randint(jax.random.fold_in(key, 12), (groups,), 0, REQ_DEV, dtype=jnp.int32)
    index_all = jnp.arange(REQUEST_TOTAL, dtype=jnp.int32)
    is_full = index_all % REQ_DEV == full_slot[index_all // REQ_DEV]
    return jnp.where(is_full, CONTEXT_SLOTS, sampled_values).astype(jnp.int32)


def incoming_keys(key):
    sampled_values = jax.random.normal(jax.random.fold_in(key, 13), (REQUEST_TOTAL, KEY_VALUE_HEADS, HEAD_DIMENSION), jnp.float32)
    return jnp.clip(sampled_values, -4.5, 4.5)


def draw_lengths(key, part):
    return request_lengths(key)


def draw_new_key(key, part):
    return incoming_keys(key).astype(jnp.bfloat16)


def draw_key_cache(key, part):
    cache_row_list = jnp.clip(jax.random.normal(jax.random.fold_in(key, 14), (REQUEST_TOTAL, KEY_VALUE_HEADS, CONTEXT_SLOTS, HEAD_DIMENSION), jnp.float32), -6.0, 6.0)
    return cache_row_list.astype(jnp.bfloat16)


def draw_queries(key, part):
    drawn = jnp.clip(jax.random.normal(jax.random.fold_in(key, 15), (REQUEST_TOTAL, QUERY_HEADS, HEAD_DIMENSION), jnp.float32), -6.0, 6.0)
    return drawn.astype(jnp.bfloat16)


def place_ends(values, key, smallest, largest):
    longest = values.shape.index(max(values.shape))
    spots = []
    for shift in (0, 1):
        where = [jax.random.randint(jax.random.fold_in(key, axis), (), 0, length) for axis, length in enumerate(values.shape)]
        where[longest] = (where[longest] + shift) % values.shape[longest]
        spots.append(tuple(where))
    return values.at[spots[0]].set(smallest).at[spots[1]].set(largest)


def block_scale(rng, shape, shards, least, largest):
    factor_of = 1.0
    for axis_at, parts in shards:
        draws = jax.random.uniform(jax.random.fold_in(jax.random.fold_in(rng, 6), axis_at), (parts,), jnp.float32, least / len(shards), largest / len(shards))
        factor_of = factor_of * jnp.repeat(jnp.exp(draws), shape[axis_at] // parts).reshape((-1,) + (1,) * (len(shape) - 1 - axis_at))
    return factor_of


def deal_out(rng, own, number, rows, number_of, top, reach, skew):
    ranking = jax.random.permutation(rng, number_of)
    crowded, common = portions_of(number_of, rows * top, reach, skew, True), portions_of(number_of, rows * top, reach, skew, False)
    places = jnp.arange(number_of)

    def named(sizes, turn):
        used = int((sizes > 0).sum())
        fixed = max(1, used // 4)
        passed = fixed + (places - fixed + turn * (used - fixed)) % max(1, number_of - fixed)
        return jnp.zeros((number_of,), jnp.int32).at[ranking[jnp.where(places < fixed, places, passed)]].set(jnp.asarray(sizes, jnp.int32))

    sizes = jnp.where(number % 4 == 0, named(crowded, number // 4), named(common, number - number // 4 - 1))
    mixed = jax.random.permutation(jax.random.fold_in(own, 3), number_of)
    donor, sink = mixed[0:number_of // 2 * 2:2], mixed[1:number_of // 2 * 2:2]
    room = jnp.minimum(sizes[donor] - 1, reach - sizes[sink]) // 2
    room = jnp.where((donor == ranking[0]) | (sink == ranking[0]) | (sizes[sink] == 0), 0, jnp.maximum(room, 0))
    passed = jax.random.randint(jax.random.fold_in(own, 4), (number_of // 2,), 0, 1 << 20) % (room + 1)
    sizes = sizes.at[donor].add(-passed).at[sink].add(passed)
    items = jnp.searchsorted(jnp.cumsum(sizes), jnp.arange(rows * top), side="right").astype(jnp.int32)
    table = items.reshape(top, rows).T
    table = table[jax.random.permutation(jax.random.fold_in(own, 1), rows)]
    turn = jax.random.randint(jax.random.fold_in(own, 2), (rows, 1), 0, top)
    return jnp.take_along_axis(table, (jnp.arange(top)[None, :] + turn) % top, axis=1)


def portions_of(number_of, total, most, lean, full):
    portions = [(1 << 20) // math.isqrt(grade ** lean) + 1 for grade in range(1, number_of + 1)]
    largest = most if full else min(most, max(-(-total // number_of), total * portions[0] // sum(portions)))
    least = 1 if total - largest >= number_of - 1 else 0
    counts, spare = [largest] + [least] * (number_of - 1), total - largest - least * (number_of - 1)
    while spare > 0:
        free = [i for i in range(1, number_of) if counts[i] < largest] or [i for i in range(1, number_of) if counts[i] < most]
        mass, remaining = sum([portions[i] for i in free]), spare
        for i in free:
            extra = min(most - counts[i], max(1, remaining * portions[i] // mass), spare)
            counts[i] = counts[i] + extra
            spare = spare - extra
    return np.array(counts)


def gaussian(stream_key, extent, width, reach, split=(), kind=jnp.bfloat16):
    gain = block_scale(stream_key, extent, split, -0.22, 0.18) if split else 1.0
    drawn = jax.random.normal(stream_key, extent, jnp.float32) * width * gain
    return jnp.minimum(jnp.maximum(drawn, -reach), reach).astype(kind)


def setup_inputs(seed: int = 0) -> dict:
    streams_of = jax.random.split(jax.random.key(seed), 17)
    queries = draw_queries(jax.random.fold_in(streams_of[16], 71), 0)
    key_cache = draw_key_cache(jax.random.fold_in(streams_of[16], 71), 0)
    stored_value_cache = gaussian(streams_of[2], (REQUEST_TOTAL, KEY_VALUE_HEADS, CONTEXT_SLOTS, HEAD_DIMENSION), 1.0, 6.0, ((0, 32), (1, 4)))
    new_key = draw_new_key(jax.random.fold_in(streams_of[16], 71), 0)
    incoming_value = gaussian(streams_of[4], (REQUEST_TOTAL, KEY_VALUE_HEADS, HEAD_DIMENSION), 1.0, 6.0, ((0, 32), (1, 4)))
    lengths = draw_lengths(jax.random.fold_in(streams_of[16], 71), 0)
    policy = place_ends(jax.random.randint(streams_of[6], (REQUEST_TOTAL, KEY_VALUE_HEADS), 0, 3), jax.random.fold_in(streams_of[6], 1), 0, 2).astype(jnp.int32)
    retained_blocks = place_ends(jax.random.randint(streams_of[7], (REQUEST_TOTAL, KEY_VALUE_HEADS, KEPT_ENTRIES), 0, BLOCK_COUNT), jax.random.fold_in(streams_of[7], 1), 0, BLOCK_COUNT - 1).astype(jnp.int32)
    out_weight = gaussian(streams_of[8], (QUERY_HEADS * HEAD_DIMENSION, D), HEAD_DIMENSION ** -0.5, 0.5, ((1, 32),))
    residual = gaussian(streams_of[9], (REQUEST_TOTAL, D), 1.0, 6.0, ((1, 32),))
    norm_gain = jnp.clip(1.0 + 0.18 * jax.random.normal(streams_of[10], (D,), jnp.float32), 0.1, 1.9)
    routes_keys = jax.random.split(jax.random.fold_in(streams_of[11], 1), REQUEST_TOTAL // REQUEST_TOTAL)
    routes_turns = jax.random.permutation(jax.random.fold_in(streams_of[11], 3), REQUEST_TOTAL // REQUEST_TOTAL)
    routes = jax.vmap(lambda own, number: deal_out(jax.random.fold_in(streams_of[11], 2), own, number, REQUEST_TOTAL, EXPERTS, TOPK, CAP, 1))(routes_keys, routes_turns).reshape((REQUEST_TOTAL, TOPK))
    router_logits = gaussian(streams_of[12], (REQUEST_TOTAL, TOPK), 1.5, 6.0, (), jnp.float32)
    gate_weight = gaussian(streams_of[13], (EXPERTS, D, FF), D ** -0.5, 0.09375, ((0, 32), (2, 4)))
    up_weight = gaussian(streams_of[14], (EXPERTS, D, FF), D ** -0.5, 0.09375, ((0, 32), (2, 4)))
    down_weight = gaussian(streams_of[15], (EXPERTS, FF, D), FF ** -0.5, 0.15625, ((0, 32), (1, 4)))
    return {"queries": queries, "key_cache": key_cache, "stored_value_cache": stored_value_cache, "new_key": new_key, "incoming_value": incoming_value, "lengths": lengths, "policy": policy, "retained_blocks": retained_blocks, "out_weight": out_weight, "residual": residual, "norm_gain": norm_gain, "routes": routes, "router_logits": router_logits, "gate_weight": gate_weight, "up_weight": up_weight, "down_weight": down_weight}


EPSILON = 1e-06

def token_keep(policy, retained_blocks, lengths):
    block_ids = jnp.arange(BLOCK_COUNT, dtype=jnp.int32)
    used_count = (lengths + BLK - 1) // BLK
    used_mask = block_ids < used_count[..., None]
    recent = block_ids >= (used_count - WIN)[..., None]
    last_block = block_ids == (used_count - 1)[..., None]
    listed = jnp.any(retained_blocks[..., :, None] == block_ids, axis=-2)
    policy_col = policy[..., None]
    block_keep = used_mask & ((policy_col == 0) & recent | (policy_col == 1) & (listed | last_block) | (policy_col == 2))
    positions = jnp.arange(CONTEXT_SLOTS, dtype=jnp.int32)
    return jnp.repeat(block_keep, BLK, axis=-1) & (positions < lengths[..., None])

def attend_request(inputs):
    query_row_list, key_rows, value_rows, own_key, own_value, kept_mask = inputs
    score_scale = HEAD_DIMENSION ** (-0.5)
    grouped_queries = query_row_list.astype(jnp.float32).reshape(KEY_VALUE_HEADS, QUERY_HEADS // KEY_VALUE_HEADS, HEAD_DIMENSION)
    scores = jnp.einsum('hqd,hkd->hqk', grouped_queries, key_rows.astype(jnp.float32)) * score_scale
    scores = jnp.where(kept_mask[:, None, :], scores, -jnp.inf)
    own_score = jnp.einsum('hqd,hd->hq', grouped_queries, own_key.astype(jnp.float32)) * score_scale
    highest = jnp.maximum(lax.optimization_barrier(jnp.max(scores, axis=-1)), own_score)
    weights = jnp.exp(scores - highest[..., None])
    own_weight = jnp.exp(own_score - highest)
    totals = lax.optimization_barrier(jnp.sum(weights, axis=-1)) + own_weight
    weights_low = lax.optimization_barrier(weights.astype(jnp.bfloat16)).astype(jnp.float32)
    own_low = lax.optimization_barrier(own_weight.astype(jnp.bfloat16)).astype(jnp.float32)
    weighted = jnp.einsum('hqk,hkd->hqd', weights_low, value_rows.astype(jnp.float32))
    weighted = weighted + own_low[..., None] * own_value.astype(jnp.float32)[:, None, :]
    return (weighted / totals[..., None]).astype(jnp.bfloat16).reshape(QUERY_HEADS * HEAD_DIMENSION)

def reference(queries, key_cache, stored_value_cache, new_key, incoming_value, lengths, policy, retained_blocks, out_weight, residual, norm_gain, routes, router_logits, gate_weight, up_weight, down_weight):
    kept_mask = token_keep(policy, retained_blocks, jnp.broadcast_to(lengths[:, None], policy.shape))
    attended = lax.map(attend_request, (queries, key_cache, stored_value_cache, new_key, incoming_value, kept_mask))
    projected = jnp.dot(attended, out_weight, preferred_element_type=jnp.float32)
    hidden = (residual.astype(jnp.float32) + projected).astype(jnp.bfloat16)
    route_flat = routes.reshape(-1).astype(jnp.int32)
    expert_ids = jnp.arange(EXPERTS, dtype=jnp.int32)
    onehot = (route_flat[:, None] == expert_ids[None, :]).astype(jnp.int32)
    route_rank = lax.optimization_barrier(jnp.sum(jnp.cumsum(onehot, axis=0) * onehot, axis=1)) - 1
    slot_index = (route_flat * CAP + route_rank).astype(jnp.int32)
    token_index = (jnp.arange(REQUEST_TOTAL * TOPK, dtype=jnp.int32) // TOPK).astype(jnp.int32)
    buffer_rows = jnp.zeros((EXPERTS * CAP, D), jnp.bfloat16).at[slot_index].set(hidden[token_index])

    def expert_apply(inputs):
        rows, gate_part, up_part, down_part = inputs
        rows_float = rows.astype(jnp.float32)
        normed = (rows_float * lax.rsqrt(lax.optimization_barrier(jnp.mean(rows_float * rows_float, axis=-1, keepdims=True)) + EPSILON) * norm_gain).astype(jnp.bfloat16)
        gate = jnp.dot(normed, gate_part, preferred_element_type=jnp.float32)
        up_proj = jnp.dot(normed, up_part, preferred_element_type=jnp.float32)
        act = (jax.nn.silu(gate) * up_proj).astype(jnp.bfloat16)
        return jnp.dot(act, down_part, preferred_element_type=jnp.float32)
    outputs = lax.map(expert_apply, (buffer_rows.reshape(EXPERTS, CAP, D), gate_weight, up_weight, down_weight))
    outputs = outputs.reshape(EXPERTS * CAP, D)
    route_weight = jax.nn.softmax(router_logits.astype(jnp.float32), axis=-1)
    picked = outputs[slot_index].reshape(REQUEST_TOTAL, TOPK, D)
    mixture = lax.optimization_barrier(jnp.sum(picked * route_weight[..., None], axis=1))
    return (hidden.astype(jnp.float32) + mixture).astype(jnp.bfloat16)
```

```python
import functools
import jax
import jax.numpy as jnp
from jax import lax
from jax.sharding import PartitionSpec as P
from jax.experimental import pallas as pl
from jax.experimental.pallas import tpu as pltpu

TOPK = 8
CAP = 64
EPSILON = 1e-06
MESH = pl.DeviceIdType.MESH
BF = jnp.bfloat16
F32 = jnp.float32


def mm(a, b, dims=((1,), (0,))):
    return lax.dot_general(a, b, (dims, ((), ())), preferred_element_type=F32)


def kernel(
    len_ref, pol_ref, ret_ref,
    q_ref, nk_ref, nv_ref, routes_ref, logit_ref, gain_ref,
    k_hbm, v_hbm, ow_hbm, res_hbm, gate_hbm, up_hbm, down_hbm,
    out_ref,
    kbuf, vbuf, pbuf, tbuf, obuf, att, attg, owb, part, recb, resb,
    hid, hg, gu, dn, ptb, psel, wcol, acc, aact,
    psib, pown, srec, qbuf, r1, tb, r2, pk, pkb, xr,
    ksem, vsem, wsem,
    sa, ra, sas, ras, sb, rb, sx, rx, sc, rc, scs, rcs, sds, rds, sd1, rd1, sd2, rd2, sf, rf,
):
    ep = lax.axis_index("ep")
    x = lax.axis_index("tp")
    c = ep % 2
    yz = ep // 2
    y = yz // 4
    z = yz % 4
    sib = (ep + 1 - 2 * c, x)

    def plane_peer(dy, dz):
        return (((y + dy) % 4 * 4 + (z + dz) % 4) * 2 + c, x)

    def x_peer(d):
        return (ep, (x + d) % 4)

    def remote(src, dst, ss, rs, dev):
        return pltpu.make_async_remote_copy(
            src_ref=src, dst_ref=dst, send_sem=ss, recv_sem=rs, device_id=dev, device_id_type=MESH
        )

    bar = pltpu.get_barrier_semaphore()

    for r in range(8):
        pltpu.make_async_copy(k_hbm.at[r], kbuf.at[r], ksem.at[r]).start()
    for r in range(8):
        pltpu.make_async_copy(v_hbm.at[r], vbuf.at[r], vsem.at[r]).start()

    def greet(d, _):
        pl.semaphore_signal(bar, inc=1, device_id=plane_peer(d // 4, d % 4), device_id_type=MESH)
        return 0

    lax.fori_loop(1, 16, greet, 0)
    pl.semaphore_signal(bar, inc=1, device_id=sib, device_id_type=MESH)
    for d in range(1, 4):
        pl.semaphore_signal(bar, inc=1, device_id=x_peer(d), device_id_type=MESH)

    weights = [
        pltpu.make_async_copy(ow_hbm.at[pl.ds(8 * x, 8), 0], owb.at[:, :, pl.ds(0, 128)], wsem.at[0]),
        pltpu.make_async_copy(ow_hbm.at[pl.ds(8 * x, 8), 1], owb.at[:, :, pl.ds(128, 128)], wsem.at[1]),
        pltpu.make_async_copy(res_hbm.at[pl.ds(64 * x, 64)], resb, wsem.at[2]),
        pltpu.make_async_copy(gate_hbm.at[0], gu.at[0, :, pl.ds(0, 384)], wsem.at[3]),
        pltpu.make_async_copy(up_hbm.at[0], gu.at[0, :, pl.ds(384, 384)], wsem.at[4]),
        pltpu.make_async_copy(gate_hbm.at[1], gu.at[1, :, pl.ds(0, 384)], wsem.at[5]),
        pltpu.make_async_copy(up_hbm.at[1], gu.at[1, :, pl.ds(384, 384)], wsem.at[6]),
        pltpu.make_async_copy(down_hbm, dn, wsem.at[7]),
    ]

    scale = 128 ** (-0.5)
    pos = lax.broadcasted_iota(jnp.int32, (1, 1024), 1)
    blk = pos >> 6
    for r in range(8):
        length = len_ref[r]
        pol = pol_ref[r]
        used = (length + 63) >> 6
        low = jnp.where(pol == 0, used - 2, jnp.where(pol == 2, 0, used - 1))
        keep = blk >= low
        for k in range(4):
            named = jnp.where(pol == 1, ret_ref[4 * r + k], -1)
            keep = keep | (blk == named)
        bias = jnp.where(keep & (pos < length), 0.0, -jnp.inf).astype(F32)
        qr = q_ref[r]
        own = jnp.sum(qr.astype(F32) * nk_ref[pl.ds(r, 1), :].astype(F32), axis=1, keepdims=True) * scale
        pltpu.make_async_copy(k_hbm.at[r], kbuf.at[r], ksem.at[r]).wait()
        s = mm(qr, kbuf[r], ((1,), (1,))) * scale + bias
        top = jnp.maximum(jnp.max(s, axis=1, keepdims=True), own)
        p = jnp.exp(s - top)
        ownw = jnp.exp(own - top)
        pbuf[r] = p.astype(BF)
        tbuf[r] = jnp.broadcast_to(jnp.sum(p, axis=1, keepdims=True) + ownw, (16, 128))
        obuf[r] = jnp.broadcast_to(ownw, (16, 128)).astype(BF)
    for w in weights[:3]:
        w.start()
    for r in range(8):
        pltpu.make_async_copy(v_hbm.at[r], vbuf.at[r], vsem.at[r]).wait()
        o = mm(pbuf[r], vbuf[r])
        o = o + obuf[r].astype(F32) * nv_ref[pl.ds(r, 1), :].astype(F32)
        att[pl.ds(16 * r, 16), :] = (o / tbuf[r]).astype(BF)
    for w in weights[3:]:
        w.start()
    rows = lax.broadcasted_iota(jnp.int32, (128, 128), 0)
    cols = lax.broadcasted_iota(jnp.int32, (128, 128), 1)
    perm = jnp.where(cols == (rows % 8) * 16 + rows // 8, 1.0, 0.0).astype(BF)
    attg[yz, c] = mm(perm, att[...]).astype(BF)

    pl.semaphore_wait(bar, 19)

    def send_a(d, _):
        remote(attg.at[yz, c], attg.at[yz, c], sa.at[d], ra.at[d], plane_peer(d // 4, d % 4)).start()
        return 0

    lax.fori_loop(1, 16, send_a, 0)
    remote(attg.at[yz, c], attg.at[yz, c], sas.at[0], ras.at[0], sib).start()

    routes = routes_ref[...]
    logits = logit_ref[...]
    grown = jnp.exp(logits - jnp.max(logits, axis=1, keepdims=True))
    rw = grown / jnp.sum(grown, axis=1, keepdims=True)
    lane = lax.broadcasted_iota(jnp.int32, (256, 128), 1)
    mems, ws = [], []
    for e in range(2):
        hit = routes == ep * 2 + e
        mems.append(jnp.sum(jnp.where(hit, 1.0, 0.0), axis=1, keepdims=True))
        ws.append(jnp.sum(jnp.where(hit, rw, 0.0), axis=1, keepdims=True))
    memb = jnp.where(lane < 64, mems[0], mems[1])
    tri = jnp.where(
        lax.broadcasted_iota(jnp.int32, (256, 256), 1) < lax.broadcasted_iota(jnp.int32, (256, 256), 0), 1.0, 0.0
    ).astype(BF)
    rank = mm(tri, memb.astype(BF))
    slot = jnp.where(lane < 64, lane, lane - 64).astype(F32)
    pt = jnp.where(rank == slot, memb, 0.0)
    psel[...] = pt.T.astype(BF)
    for e in range(2):
        inside = (lane < 64) if e == 0 else (lane >= 64)
        ptb[e] = jnp.where(inside, pt, 0.0).astype(BF)
        wcol[e] = jnp.broadcast_to(ws[e], (256, 128))

    def pass_a(d, _):
        src = (y + 4 - d // 4) % 4 * 4 + (z + 4 - d % 4) % 4
        remote(attg.at[src, c], attg.at[src, c], sa.at[d], ra.at[d], sib).wait_recv()
        remote(attg.at[src, c], attg.at[src, c], sas.at[d], ras.at[d], sib).start()
        return 0

    lax.fori_loop(1, 16, pass_a, 0)

    weights[0].wait()
    weights[1].wait()

    def project(cc):
        total = jnp.zeros((256, 256), F32)
        for g in range(8):
            lhs = attg[:, cc, pl.ds(16 * g, 16), :].reshape(256, 128)
            total = total + mm(lhs, owb[g])
        total = total.reshape(16, 16, 256)
        part[:, cc] = total[:, :8, :128] + total[:, 8:, 128:]

    project(c)

    def got_a(d, _):
        src = (y + 4 - d // 4) % 4 * 4 + (z + 4 - d % 4) % 4
        remote(attg.at[src, 1 - c], attg.at[src, 1 - c], sas.at[d], ras.at[d], sib).wait_recv()
        return 0

    lax.fori_loop(0, 16, got_a, 0)
    project(1 - c)

    for d in range(1, 4):
        to = (x + d) % 4
        remote(part.at[pl.ds(4 * to, 4)], recb.at[d], sb.at[d], rb.at[d], x_peer(d)).start()
    weights[2].wait()
    total = part[pl.ds(4 * x, 4)].reshape(64, 128)
    for d in range(1, 4):
        remote(recb.at[d], recb.at[d], sb.at[d], rb.at[d], x_peer(d)).wait_recv()
        total = total + recb[d].reshape(64, 128)
    mine = pl.ds(pl.multiple_of(64 * x, 64), 64)
    hid[yz, c, mine, :] = (resb[...].astype(F32) + total).astype(BF)

    for d in range(1, 4):
        remote(hid.at[yz, c, mine], hid.at[yz, c, mine], sx.at[d], rx.at[d], x_peer(d)).start()
    for d in range(1, 4):
        there = pl.ds(pl.multiple_of(64 * ((x + 4 - d) % 4), 64), 64)
        remote(hid.at[yz, c, there], hid.at[yz, c, there], sx.at[d], rx.at[d], x_peer(d)).wait_recv()

    def first_axis(d):
        return plane_peer(d * c, d * (1 - c))

    def second_axis(d):
        return plane_peer(d * (1 - c), d * c)

    def origin(d1, d2):
        dy = d1 * c + d2 * (1 - c)
        dz = d1 * (1 - c) + d2 * c
        return (y + 4 - dy) % 4 * 4 + (z + 4 - dz) % 4, dy * 4 + dz

    def copy_c(src, d1, d2, dev):
        return remote(hid.at[src, c], hid.at[src, c], sc.at[4 * d1 + d2], rc.at[4 * d1 + d2], dev)

    def got_plane(d1, d2):
        copy_c(origin(d1, d2)[0], d1, d2, sib).wait_recv()

    def copy_cs(d1, d2):
        src, at = origin(d1, d2)
        return remote(hid.at[src, c], hid.at[src, c], scs.at[at], rcs.at[at], sib)

    for d in range(1, 4):
        copy_c(yz, d, 0, first_axis(d)).start()
    for d1 in range(4):
        if d1:
            got_plane(d1, 0)
        for d2 in range(1, 4):
            copy_c(origin(d1, 0)[0], d1, d2, second_axis(d2)).start()
        copy_cs(d1, 0).start()

    lane64 = lax.broadcasted_iota(jnp.int32, (64, 128), 1) // 32

    def pack(value, j):
        out = jnp.zeros((64, 128), F32)
        for k in range(4):
            piece = value[64 * k : 64 * k + 64]
            shift = (32 * (k - j)) % 128
            if shift:
                piece = pltpu.roll(piece, shift, 1)
            out = jnp.where(lane64 == k, piece, out)
        return out

    block = hid[yz, c].astype(F32)
    for j in range(4):
        pk[j] = pack(block, j)
    base = pk[x]

    def pass_c(n, _):
        d1, d2 = n % 4, n // 4
        got_plane(d1, d2)
        copy_cs(d1, d2).start()
        return 0

    lax.fori_loop(4, 16, pass_c, 0)

    def got_c(at, _):
        src = (y + 4 - at // 4) % 4 * 4 + (z + 4 - at % 4) % 4
        remote(hid.at[src, 1 - c], hid.at[src, 1 - c], scs.at[at], rcs.at[at], sib).wait_recv()
        return 0

    lax.fori_loop(0, 16, got_c, 0)

    def pick(b, squares):
        for h in range(2):
            rows_of = mm(psel[...], hid[b, h])
            squares = squares + rows_of * rows_of
            at = pl.multiple_of((2 * b + h) * 128, 128)
            hg[:, pl.ds(at, 128)] = (rows_of * gain_ref[pl.ds(2 * b + h, 1), :]).astype(BF)
        return squares

    squares = lax.fori_loop(0, 16, pick, jnp.zeros((128, 128), F32))
    rs = lax.rsqrt(jnp.sum(squares, axis=1, keepdims=True) / 4096 + EPSILON)
    for w in weights[3:]:
        w.wait()
    for e in range(2):
        for n in range(3):
            acc[e, :, pl.ds(256 * n, 256)] = mm(hg[pl.ds(64 * e, 64), :], gu[e, :, pl.ds(256 * n, 256)])
    halves = []
    for e in range(2):
        re = rs[64 * e : 64 * e + 64]
        gate = acc[e, :, pl.ds(0, 384)] * re
        up = acc[e, :, pl.ds(384, 384)] * re
        halves.append((gate / (1.0 + jnp.exp(-gate)) * up).astype(BF))
    act = jnp.concatenate(halves, axis=0)
    for e in range(2):
        spread = mm(ptb[e], act)
        aact[:, pl.ds(384 * e, 384)] = (spread * wcol[e][:, :1]).astype(BF)

    def dest(n, cc):
        i1 = n // 4
        d1 = jnp.where(i1 == 0, 2, jnp.where(i1 == 1, 1, jnp.where(i1 == 2, 3, 0)))
        d2 = n % 4
        dy = d1 * (1 - cc) + d2 * cc
        dz = d2 * (1 - cc) + d1 * cc
        return d1, d2, (y + dy) % 4 * 4 + (z + dz) % 4

    def down(n):
        _, _, mine_at = dest(n, c)
        _, _, sib_at = dest(n, 1 - c)
        mine_col = pl.multiple_of((2 * mine_at + c) * 128, 128)
        sib_col = pl.multiple_of((2 * sib_at + 1 - c) * 128, 128)
        rhs = jnp.concatenate([dn[:, pl.ds(sib_col, 128)], dn[:, pl.ds(mine_col, 128)]], axis=1)
        got = mm(aact[...], rhs)
        psib[n] = got[:, :128].astype(BF)
        pown[n] = got[:, 128:]
        remote(psib.at[n], srec.at[n], sds.at[n], rds.at[n], sib).start()

    def join(n):
        remote(psib.at[n], srec.at[n], sds.at[n], rds.at[n], sib).wait_recv()
        return pown[n] + srec[n].astype(F32)

    def copy_d1(n):
        d1, d2, _ = dest(n, c)
        dev = plane_peer(d1 * (1 - c), d1 * c)
        return remote(qbuf.at[n], r1.at[n], sd1.at[n], rd1.at[n], dev)

    def forward(n):
        qbuf[n] = join(n).astype(BF)
        copy_d1(n).start()

    down(0)

    def step(n, _):
        down(n)
        forward(n - 1)
        return 0

    lax.fori_loop(1, 13, step, 0)
    for n in range(13, 16):
        down(n)

    def copy_d2(d2):
        return remote(tb.at[d2], r2.at[d2], sd2.at[d2], rd2.at[d2], plane_peer(d2 * c, d2 * (1 - c)))

    for d2 in (2, 1, 3, 0):
        total = join(12 + d2)
        for i1 in range(3):
            n = 4 * i1 + d2
            copy_d1(n).wait_recv()
            total = total + r1[n].astype(F32)
        if d2:
            tb[d2] = total.astype(BF)
            copy_d2(d2).start()
    for d2 in (1, 3, 2):
        copy_d2(d2).wait_recv()
        total = total + r2[d2].astype(F32)

    for j in range(4):
        packed = pack(total, j)
        pk[j] = packed
        pkb[j] = packed.astype(BF)
    copies = []
    for d in (2, 1, 3):
        cp = remote(pkb.at[(x + d) % 4], xr.at[d], sf.at[d], rf.at[d], x_peer(d))
        cp.start()
        copies.append(cp)
    total = pk[x]
    for d in (1, 3, 2):
        remote(xr.at[d], xr.at[d], sf.at[d], rf.at[d], x_peer(d)).wait_recv()
        total = total + xr[d].astype(F32)
    total = (base + total).astype(BF)
    for k in range(4):
        out_ref[pl.ds(64 * k, 64), :] = total[:, 32 * k : 32 * k + 32]

    def drain_plane(d, _):
        remote(attg.at[yz, c], attg.at[yz, c], sa.at[d], ra.at[d], sib).wait_send()
        copy_c(yz, d // 4, d % 4, sib).wait_send()
        return 0

    def drain_sib(d, _):
        remote(attg.at[yz, c], attg.at[yz, c], sas.at[d], ras.at[d], sib).wait_send()
        remote(hid.at[yz, c], hid.at[yz, c], scs.at[d], rcs.at[d], sib).wait_send()
        remote(psib.at[d], srec.at[d], sds.at[d], rds.at[d], sib).wait_send()
        return 0

    def drain_d1(n, _):
        copy_d1(n).wait_send()
        return 0

    lax.fori_loop(1, 16, drain_plane, 0)
    lax.fori_loop(0, 16, drain_sib, 0)
    lax.fori_loop(0, 12, drain_d1, 0)
    for d in range(1, 4):
        remote(part.at[pl.ds(4 * ((x + d) % 4), 4)], recb.at[d], sb.at[d], rb.at[d], x_peer(d)).wait_send()
        remote(hid.at[yz, c, mine], hid.at[yz, c, mine], sx.at[d], rx.at[d], x_peer(d)).wait_send()
        copy_d2(d).wait_send()
    for cp in copies:
        cp.wait_send()


def per_device(
    queries, key_cache, stored_value_cache, new_key, incoming_value, lengths, policy, retained_blocks,
    out_weight, residual, norm_gain, routes, router_logits, gate_weight, up_weight, down_weight,
):
    vm = pl.BlockSpec(memory_space=pltpu.VMEM)
    sm = pl.BlockSpec(memory_space=pltpu.SMEM)
    hb = pl.BlockSpec(memory_space=pl.ANY)
    dma = pltpu.SemaphoreType.DMA
    scratch = [
        pltpu.VMEM((8, 1024, 128), BF),
        pltpu.VMEM((8, 1024, 128), BF),
        pltpu.VMEM((8, 16, 1024), BF),
        pltpu.VMEM((8, 16, 128), F32),
        pltpu.VMEM((8, 16, 128), BF),
        pltpu.VMEM((128, 128), BF),
        pltpu.VMEM((16, 2, 128, 128), BF),
        pltpu.VMEM((8, 128, 256), BF),
        pltpu.VMEM((16, 2, 8, 128), F32),
        pltpu.VMEM((4, 4, 2, 8, 128), F32),
        pltpu.VMEM((64, 128), BF),
        pltpu.VMEM((16, 2, 256, 128), BF),
        pltpu.VMEM((128, 4096), BF),
        pltpu.VMEM((2, 4096, 768), BF),
        pltpu.VMEM((768, 4096), BF),
        pltpu.VMEM((2, 256, 128), BF),
        pltpu.VMEM((128, 256), BF),
        pltpu.VMEM((2, 256, 128), F32),
        pltpu.VMEM((2, 64, 768), F32),
        pltpu.VMEM((256, 768), BF),
        pltpu.VMEM((16, 256, 128), BF),
        pltpu.VMEM((16, 256, 128), F32),
        pltpu.VMEM((16, 256, 128), BF),
        pltpu.VMEM((12, 256, 128), BF),
        pltpu.VMEM((12, 256, 128), BF),
        pltpu.VMEM((4, 256, 128), BF),
        pltpu.VMEM((4, 256, 128), BF),
        pltpu.VMEM((4, 64, 128), F32),
        pltpu.VMEM((4, 64, 128), BF),
        pltpu.VMEM((4, 64, 128), BF),
        dma((8,)), dma((8,)), dma((8,)),
        dma((16,)), dma((16,)), dma((16,)), dma((16,)),
        dma((4,)), dma((4,)), dma((4,)), dma((4,)),
        dma((16,)), dma((16,)), dma((16,)), dma((16,)),
        dma((16,)), dma((16,)), dma((12,)), dma((12,)),
        dma((4,)), dma((4,)), dma((4,)), dma((4,)),
    ]
    return pl.pallas_call(
        kernel,
        out_shape=jax.ShapeDtypeStruct((256, 32), BF),
        in_specs=[sm] * 3 + [vm] * 6 + [hb] * 7,
        out_specs=vm,
        scratch_shapes=scratch,
        name="decode_step",
        cost_estimate=pl.CostEstimate(flops=3_000_000_000, bytes_accessed=26_000_000, transcendentals=200_000),
        compiler_params=pltpu.CompilerParams(
            collective_id=0, has_side_effects=True, vmem_limit_bytes=56 * 2**20
        ),
    )(
        lengths, policy.reshape(8), retained_blocks.reshape(32),
        queries, new_key.reshape(8, 128), incoming_value.reshape(8, 128),
        routes, router_logits, norm_gain.reshape(32, 128),
        key_cache.reshape(8, 1024, 128), stored_value_cache.reshape(8, 1024, 128),
        out_weight.reshape(32, 2, 128, 128), residual,
        gate_weight, up_weight, down_weight.reshape(768, 4096),
    )


def solution(mesh):
    return jax.shard_map(
        per_device,
        mesh=mesh,
        in_specs=(
            P("ep", "tp", None),
            P("ep", "tp", None, None),
            P("ep", "tp", None, None),
            P("ep", "tp", None),
            P("ep", "tp", None),
            P("ep"),
            P("ep", "tp"),
            P("ep", "tp", None),
            P(None, "ep"),
            P(None, "ep"),
            P(),
            P(),
            P(),
            P("ep", None, "tp"),
            P("ep", None, "tp"),
            P("ep", "tp", None),
        ),
        out_specs=P(None, ("ep", "tp")),
        check_vma=False,
    )
```

```python
import functools
import jax
import jax.numpy as jnp
from jax import lax
from jax.sharding import PartitionSpec as P
from jax.experimental import pallas as pl
from jax.experimental.pallas import tpu as pltpu

TOPK = 8
CAP = 64
EPSILON = 1e-06
MESH = pl.DeviceIdType.MESH
BF = jnp.bfloat16
F32 = jnp.float32


def mm(a, b, dims=((1,), (0,))):
    return lax.dot_general(a, b, (dims, ((), ())), preferred_element_type=F32)


def kernel(
    len_hbm, pol_hbm, ret_hbm, q_hbm, nk_hbm, nv_hbm, routes_hbm, logit_hbm, gain_hbm,
    k_hbm, v_hbm, ow_hbm, res_hbm, gate_hbm, up_hbm, down_hbm,
    out_ref,
    len_ref, pol_ref, ret_ref, q_ref, nk_ref, nv_ref, routes_ref, logit_ref, gain_ref,
    kbuf, vbuf, pbuf, tbuf, obuf, att, attg, owb, pb, nat, resb,
    hid, sq, gu, dn, ptb, psel, wcol, acc, aact,
    psib, pown, srec, qbuf, r1, tb, last, block, r2,
    small, ksem, vsem, wsem,
    sa, ra, sas, ras, sb, rb, sc, rc, scs, rcs, sds, rds, sd1, rd1, sd2, rd2,
):
    ep = lax.axis_index("ep")
    x = lax.axis_index("tp")
    c = ep % 2
    yz = ep // 2
    y = yz // 4
    z = yz % 4
    a1 = z * (1 - c) + y * c
    a2 = y * (1 - c) + z * c
    sib = (ep + 1 - 2 * c, x)
    near = (1, 3, 2)

    def peer(dx, dy, dz):
        return (((y + dy) % 4 * 4 + (z + dz) % 4) * 2 + c, (x + dx) % 4)

    def over_axis1(d):
        return peer(0, d * c, d * (1 - c))

    def over_axis2(d, dx=0):
        return peer(dx, d * (1 - c), d * c)

    def remote(src, dst, ss, rs, dev):
        return pltpu.make_async_remote_copy(
            src_ref=src, dst_ref=dst, send_sem=ss, recv_sem=rs, device_id=dev, device_id_type=MESH
        )

    def sent(ref, sem):
        remote(ref, ref, sem, rb.at[0], sib).wait_send()

    def got(ref, sem):
        remote(ref, ref, sb.at[0], sem, sib).wait_recv()

    bar = pltpu.get_barrier_semaphore()
    partners = [sib] + [peer(d, 0, 0) for d in near] + [peer(0, d, 0) for d in near] + [peer(0, 0, d) for d in near]
    for dev in partners:
        pl.semaphore_signal(bar, inc=1, device_id=dev, device_id_type=MESH)

    smalls = [
        pltpu.make_async_copy(src, dst, small.at[i])
        for i, (src, dst) in enumerate((
            (routes_hbm, routes_ref), (logit_hbm, logit_ref),
            (len_hbm, len_ref), (pol_hbm, pol_ref), (ret_hbm, ret_ref),
            (q_hbm, q_ref), (nk_hbm, nk_ref), (nv_hbm, nv_ref), (gain_hbm, gain_ref),
        ))
    ]
    for cp in smalls:
        cp.start()
    for r in range(8):
        pltpu.make_async_copy(k_hbm.at[r], kbuf.at[r], ksem.at[r]).start()
    for r in range(8):
        pltpu.make_async_copy(v_hbm.at[r], vbuf.at[r], vsem.at[r]).start()
    weights = [
        pltpu.make_async_copy(ow_hbm.at[pl.ds(8 * x, 8), 0], owb.at[:, :, pl.ds(0, 128)], wsem.at[0]),
        pltpu.make_async_copy(ow_hbm.at[pl.ds(8 * x, 8), 1], owb.at[:, :, pl.ds(128, 128)], wsem.at[1]),
        pltpu.make_async_copy(res_hbm, resb, wsem.at[2]),
        pltpu.make_async_copy(gate_hbm.at[0], gu.at[0, :, pl.ds(0, 384)], wsem.at[3]),
        pltpu.make_async_copy(up_hbm.at[0], gu.at[0, :, pl.ds(384, 384)], wsem.at[4]),
        pltpu.make_async_copy(gate_hbm.at[1], gu.at[1, :, pl.ds(0, 384)], wsem.at[5]),
        pltpu.make_async_copy(up_hbm.at[1], gu.at[1, :, pl.ds(384, 384)], wsem.at[6]),
        pltpu.make_async_copy(down_hbm, dn, wsem.at[7]),
    ]

    for cp in smalls:
        cp.wait()

    logits = logit_ref[...]
    grown = jnp.exp(logits - jnp.max(logits, axis=0, keepdims=True))
    rw = grown / jnp.sum(grown, axis=0, keepdims=True)
    sub = lax.broadcasted_iota(jnp.int32, (128, 256), 0)
    mem, wrow = [], []
    for e in range(2):
        hit = routes_ref[...] == ep * 2 + e
        mem.append(jnp.sum(jnp.where(hit, 1.0, 0.0), axis=0, keepdims=True))
        wrow.append(jnp.sum(jnp.where(hit, rw, 0.0), axis=0, keepdims=True))
    memb = jnp.where(sub < 64, mem[0], mem[1])
    tri = jnp.where(
        lax.broadcasted_iota(jnp.int32, (256, 256), 0) < lax.broadcasted_iota(jnp.int32, (256, 256), 1), 1.0, 0.0
    ).astype(BF)
    rank = mm(memb.astype(BF), tri)
    slot = jnp.where(sub < 64, sub, sub - 64).astype(F32)
    chosen = jnp.where(rank == slot, memb, 0.0)
    psel[...] = chosen.astype(BF)
    spread_t = chosen.T
    weight_t = (chosen * jnp.where(sub < 64, wrow[0], wrow[1])).T
    lane = lax.broadcasted_iota(jnp.int32, (256, 128), 1)
    for e in range(2):
        inside = (lane < 64) if e == 0 else (lane >= 64)
        ptb[e] = jnp.where(inside, spread_t, 0.0).astype(BF)
        wcol[e] = jnp.broadcast_to(jnp.sum(jnp.where(inside, weight_t, 0.0), axis=1, keepdims=True), (256, 128))

    scale = 128 ** (-0.5)
    pos = lax.broadcasted_iota(jnp.int32, (1, 1024), 1)
    blk = pos >> 6
    for r in range(8):
        length = len_ref[r]
        pol = pol_ref[r]
        used = (length + 63) >> 6
        low = jnp.where(pol == 0, used - 2, jnp.where(pol == 2, 0, used - 1))
        keep = blk >= low
        for k in range(4):
            named = jnp.where(pol == 1, ret_ref[k, r], -1)
            keep = keep | (blk == named)
        bias = jnp.where(keep & (pos < length), 0.0, -jnp.inf).astype(F32)
        qr = q_ref[r]
        own = jnp.sum(qr.astype(F32) * nk_ref[pl.ds(r, 1), :].astype(F32), axis=1, keepdims=True) * scale
        pltpu.make_async_copy(k_hbm.at[r], kbuf.at[r], ksem.at[r]).wait()
        s = mm(qr, kbuf[r], ((1,), (1,))) * scale + bias
        top = jnp.maximum(jnp.max(s, axis=1, keepdims=True), own)
        p = jnp.exp(s - top)
        ownw = jnp.exp(own - top)
        pbuf[r] = p.astype(BF)
        tbuf[r] = jnp.broadcast_to(jnp.sum(p, axis=1, keepdims=True) + ownw, (16, 128))
        obuf[r] = jnp.broadcast_to(ownw, (16, 128)).astype(BF)
    for w in weights[:3]:
        w.start()
    for r in range(8):
        pltpu.make_async_copy(v_hbm.at[r], vbuf.at[r], vsem.at[r]).wait()
        o = mm(pbuf[r], vbuf[r])
        o = o + obuf[r].astype(F32) * nv_ref[pl.ds(r, 1), :].astype(F32)
        att[pl.ds(16 * r, 16), :] = (o / tbuf[r]).astype(BF)
    for w in weights[3:]:
        w.start()
    rows = lax.broadcasted_iota(jnp.int32, (128, 128), 0)
    cols = lax.broadcasted_iota(jnp.int32, (128, 128), 1)
    perm = jnp.where(cols == (rows % 8) * 16 + rows // 8, 1.0, 0.0).astype(BF)
    here = 4 * a2 + a1
    attg[c, here] = mm(perm, att[...]).astype(BF)

    pl.semaphore_wait(bar, len(partners))

    class Gather:
        def __init__(self, buf, sends, gets, sib_sends, sib_gets):
            self.buf, self.sends, self.gets = buf, sends, gets
            self.sib_sends, self.sib_gets = sib_sends, sib_gets

        def row(self, d2, cc):
            base = a2 if cc is c else a1
            return self.buf.at[cc, pl.ds(4 * ((base + 4 - d2) % 4), 4)]

        def send(self, d1, get, dev):
            at = self.buf.at[c, 4 * a2 + (a1 + 4 - d1) % 4]
            remote(at, at, self.sends.at[0], self.gets.at[get], dev).start()

        def over(self, d2):
            at = self.row(d2, c)
            remote(at, at, self.sib_sends.at[0], self.sib_gets.at[d2], sib).start()

        def start(self):
            for d in near:
                self.send(0, 4 + d, over_axis1(d))
            for d in near:
                self.send(0, d, over_axis2(d))

        def relay(self):
            for d1 in near:
                got(self.buf.at[c, 4 * a2 + (a1 + 4 - d1) % 4], self.gets.at[4 + d1])
                for d2 in near:
                    self.send(d1, d2, over_axis2(d2))
            self.over(0)

        def pass_on(self, d2):
            got(self.row(d2, c), self.gets.at[d2])
            self.over(d2)

        def arrived(self, d2):
            got(self.row(d2, 1 - c), self.sib_gets.at[d2])

        def finish(self):
            sent(self.buf.at[c, pl.ds(0, 15)], self.sends.at[0])
            sent(self.buf.at[c], self.sib_sends.at[0])

    attended = Gather(attg, sa, ra, sas, ras)
    attended.start()
    attended.relay()
    for d in near:
        attended.pass_on(d)

    weights[0].wait()
    weights[1].wait()

    def project(cc, half):
        total = jnp.zeros((256, 256), F32)
        for g in range(8):
            lhs = attg[cc, :, pl.ds(16 * g, 16), :].reshape(256, 128)
            total = total + mm(lhs, owb[g])
        total = total.reshape(16, 16, 256)
        total = total[:, :8, :128] + total[:, 8:, 128:]
        pb[x, cc] = total.reshape(128, 128).astype(BF)
        for d in near:
            remote(pb.at[x, cc], pb.at[x, cc], sb.at[0], rb.at[2 * d + half], peer(d, 0, 0)).start()

    project(c, 0)
    for d in (0,) + near:
        attended.arrived(d)
    project(1 - c, 1)
    attended.finish()
    weights[2].wait()
    for half, cc in ((0, c), (1, 1 - c)):
        for d in near:
            got(pb.at[(x + 4 - d) % 4, cc], rb.at[2 * d + half])
    for cc in range(2):
        total = pb[0, cc].astype(F32)
        for j in range(1, 4):
            total = total + pb[j, cc].astype(F32)
        total = total.reshape(16, 8, 128)
        for at in range(16):
            nat[at if cc == 0 else at % 4 * 4 + at // 4, cc] = total[at]
    hid[c, here] = (resb[...].astype(F32) + nat[...].reshape(256, 128)).astype(BF)

    hidden = Gather(hid, sc, rc, scs, rcs)
    hidden.start()
    sent(pb.at[pl.ds(0, 3)], sb.at[0])
    block[...] = hid[c, here].astype(F32).T
    hidden.relay()
    for w in weights[3:]:
        w.wait()

    def products(d2, cc, first):
        row = ((a2 if cc is c else a1) + 4 - d2) % 4
        at = [(4 * row + k) * (1 - cc) + (4 * k + row) * cc for k in range(4)]
        picked = mm(psel[...], jnp.concatenate([hid[cc, 4 * row + k] for k in range(4)], axis=1))
        squares = picked * picked
        gain = jnp.concatenate([gain_ref[pl.ds(2 * b + cc, 1), :] for b in at], axis=1)
        squares = squares[:, :128] + squares[:, 128:256] + squares[:, 256:384] + squares[:, 384:]
        lhs = (picked * gain).astype(BF)
        cols = [pl.ds(pl.multiple_of((2 * b + cc) * 128, 128), 128) for b in at]
        for e in range(2):
            rhs = jnp.concatenate([gu[e, col, :] for col in cols], axis=0)
            part = mm(lhs[64 * e : 64 * e + 64], rhs)
            acc[e] = part if first else acc[e] + part
        sq[...] = squares if first else sq[...] + squares

    products(0, c, True)
    waiting = 0
    for d2 in near:
        hidden.pass_on(d2)
        hidden.arrived(waiting)
        products(waiting, 1 - c, False)
        products(d2, c, False)
        waiting = d2
    hidden.arrived(waiting)
    products(waiting, 1 - c, False)
    rs = lax.rsqrt(jnp.sum(sq[...], axis=1, keepdims=True) / 4096 + EPSILON)
    halves = []
    for e in range(2):
        re = rs[64 * e : 64 * e + 64]
        gate = acc[e, :, pl.ds(0, 384)] * re
        up = acc[e, :, pl.ds(384, 384)] * re
        halves.append((gate / (1.0 + jnp.exp(-gate)) * up).astype(BF))
    act = jnp.concatenate(halves, axis=0)
    for e in range(2):
        spread = mm(ptb[e], act)
        aact[:, pl.ds(384 * e, 384)] = (spread * wcol[e][:, :1]).astype(BF)

    def dest(n, cc):
        i1 = n // 4
        d1 = jnp.where(i1 == 0, 2, jnp.where(i1 == 1, 1, jnp.where(i1 == 2, 3, 0)))
        d2 = n % 4
        dy = d1 * (1 - cc) + d2 * cc
        dz = d2 * (1 - cc) + d1 * cc
        return d1, d2, (y + dy) % 4 * 4 + (z + dz) % 4

    def down(n):
        mine_col = pl.multiple_of((2 * dest(n, c)[2] + c) * 128, 128)
        sib_col = pl.multiple_of((2 * dest(n, 1 - c)[2] + 1 - c) * 128, 128)
        rhs = jnp.concatenate([dn[:, pl.ds(sib_col, 128)], dn[:, pl.ds(mine_col, 128)]], axis=1)
        both = mm(aact[...], rhs)
        psib[n] = both[:, :128].astype(BF)
        remote(psib.at[n], srec.at[n], sds.at[0], rds.at[n], sib).start()
        pown[n] = both[:, 128:]

    def join(n):
        got(srec.at[n], rds.at[n])
        return pown[n] + srec[n].astype(F32)

    def forward(n):
        d1, d2, _ = dest(n, c)
        qbuf[n] = join(n).astype(BF)
        to = r1.at[d2, n // 4]
        remote(qbuf.at[n], to, sd1.at[0], rd1.at[d2], peer(0, d1 * (1 - c), d1 * c)).start()

    down(0)

    def step(n, _):
        down(n)
        forward(n - 1)
        return 0

    lax.fori_loop(1, 13, step, 0)
    for n in range(13, 16):
        down(n)
    hidden.finish()

    def slab(j):
        return pl.ds(pl.multiple_of(32 * (j % 4), 32), 32)

    for d2 in (2, 1, 3, 0):
        total = join(12 + d2)
        got(r1.at[d2], rd1.at[d2])
        for i1 in range(3):
            total = total + r1[d2, i1].astype(F32)
        turned = total.T
        tb[d2] = turned.astype(BF)
        if d2 == 0:
            last[...] = block[slab(x), :] + jnp.where(x == 0, turned[:32], jnp.where(x == 1, turned[32:64], jnp.where(x == 2, turned[64:96], turned[96:])))
        for dx in (2, 1, 3, 0):
            if d2 or dx:
                dev = peer(dx, d2 * c, d2 * (1 - c))
                remote(tb.at[d2, slab(x + dx)], r2.at[4 * d2 + dx], sd2.at[0], rd2.at[0], dev).start()
    sent(psib, sds.at[0])
    sent(qbuf, sd1.at[0])
    got(r2.at[pl.ds(1, 15)], rd2.at[0])
    total = last[...]
    for k in range(1, 16):
        total = total + r2[k].astype(F32)
    out_ref[...] = total.astype(BF)
    sent(r2.at[pl.ds(1, 15)], sd2.at[0])


def per_device(
    queries, key_cache, stored_value_cache, new_key, incoming_value, lengths, policy, retained_blocks,
    out_weight, residual, norm_gain, routes, router_logits, gate_weight, up_weight, down_weight,
):
    vm = pl.BlockSpec(memory_space=pltpu.VMEM)
    hb = pl.BlockSpec(memory_space=pl.ANY)
    dma = pltpu.SemaphoreType.DMA
    scratch = [
        pltpu.SMEM((8,), jnp.int32),
        pltpu.SMEM((8,), jnp.int32),
        pltpu.SMEM((4, 8), jnp.int32),
        pltpu.VMEM((8, 16, 128), BF),
        pltpu.VMEM((8, 128), BF),
        pltpu.VMEM((8, 128), BF),
        pltpu.VMEM((8, 256), jnp.int32),
        pltpu.VMEM((8, 256), F32),
        pltpu.VMEM((32, 128), F32),
        pltpu.VMEM((8, 1024, 128), BF),
        pltpu.VMEM((8, 1024, 128), BF),
        pltpu.VMEM((8, 16, 1024), BF),
        pltpu.VMEM((8, 16, 128), F32),
        pltpu.VMEM((8, 16, 128), BF),
        pltpu.VMEM((128, 128), BF),
        pltpu.VMEM((2, 16, 128, 128), BF),
        pltpu.VMEM((8, 128, 256), BF),
        pltpu.VMEM((4, 2, 128, 128), BF),
        pltpu.VMEM((16, 2, 8, 128), F32),
        pltpu.VMEM((256, 128), BF),
        pltpu.VMEM((2, 16, 256, 128), BF),
        pltpu.VMEM((128, 128), F32),
        pltpu.VMEM((2, 4096, 768), BF),
        pltpu.VMEM((768, 4096), BF),
        pltpu.VMEM((2, 256, 128), BF),
        pltpu.VMEM((128, 256), BF),
        pltpu.VMEM((2, 256, 128), F32),
        pltpu.VMEM((2, 64, 768), F32),
        pltpu.VMEM((256, 768), BF),
        pltpu.VMEM((16, 256, 128), BF),
        pltpu.VMEM((16, 256, 128), F32),
        pltpu.VMEM((16, 256, 128), BF),
        pltpu.VMEM((12, 256, 128), BF),
        pltpu.VMEM((4, 3, 256, 128), BF),
        pltpu.VMEM((4, 128, 256), BF),
        pltpu.VMEM((32, 256), F32),
        pltpu.VMEM((128, 256), F32),
        pltpu.VMEM((16, 32, 256), BF),
        dma((9,)), dma((8,)), dma((8,)), dma((8,)),
        dma((1,)), dma((8,)), dma((1,)), dma((4,)),
        dma((1,)), dma((8,)),
        dma((1,)), dma((8,)), dma((1,)), dma((4,)),
        dma((1,)), dma((16,)), dma((1,)), dma((4,)),
        dma((1,)), dma((1,)),
    ]
    return pl.pallas_call(
        kernel,
        out_shape=jax.ShapeDtypeStruct((32, 256), BF),
        in_specs=[hb] * 16,
        out_specs=vm,
        scratch_shapes=scratch,
        name="decode_step",
        cost_estimate=pl.CostEstimate(flops=3_000_000_000, bytes_accessed=26_000_000, transcendentals=200_000),
        compiler_params=pltpu.CompilerParams(
            collective_id=0, has_side_effects=True, vmem_limit_bytes=56 * 2**20
        ),
    )(
        lengths, policy.reshape(8), retained_blocks.transpose(1, 2, 0).reshape(4, 8),
        queries, new_key.reshape(8, 128), incoming_value.reshape(8, 128),
        routes.T, router_logits.T, norm_gain.reshape(32, 128),
        key_cache.reshape(8, 1024, 128), stored_value_cache.reshape(8, 1024, 128),
        out_weight.reshape(32, 2, 128, 128), residual,
        gate_weight, up_weight, down_weight.reshape(768, 4096),
    ).T


def solution(mesh):
    return jax.shard_map(
        per_device,
        mesh=mesh,
        in_specs=(
            P("ep", "tp", None),
            P("ep", "tp", None, None),
            P("ep", "tp", None, None),
            P("ep", "tp", None),
            P("ep", "tp", None),
            P("ep"),
            P("ep", "tp"),
            P("ep", "tp", None),
            P(None, "ep"),
            P(None, "ep"),
            P(),
            P(),
            P(),
            P("ep", None, "tp"),
            P("ep", None, "tp"),
            P("ep", "tp", None),
        ),
        out_specs=P(None, ("ep", "tp")),
        check_vma=False,
    )
```

```python
import functools
import jax
import jax.numpy as jnp
from jax import lax
from jax.sharding import PartitionSpec as P
from jax.experimental import pallas as pl
from jax.experimental.pallas import tpu as pltpu

TOPK = 8
CAP = 64
EPSILON = 1e-06
MESH = pl.DeviceIdType.MESH
BF = jnp.bfloat16
F32 = jnp.float32


def mm(a, b, dims=((1,), (0,))):
    return lax.dot_general(a, b, (dims, ((), ())), preferred_element_type=F32)


def kernel(
    len_hbm, pol_hbm, ret_hbm, q_hbm, nk_hbm, nv_hbm, routes_hbm, logit_hbm, gain_hbm,
    k_hbm, v_hbm, ow_hbm, res_hbm, gate_hbm, up_hbm, down_hbm,
    out_ref,
    len_ref, pol_ref, ret_ref, q_ref, nk_ref, nv_ref, routes_ref, logit_ref, gain_ref,
    kbuf, vbuf, pbuf, tbuf, obuf, att, attg, owb, pb, nat, resb,
    hid, sq, gu, dn, ptb, psel, wcol, acc, aact,
    psib, pown, srec, qbuf, r1, tb, last, block, r2,
    small, ksem, vsem, wsem,
    sa, ra, sas, ras, sb, rb, sc, rc, scs, rcs, sds, rds, sd1, rd1, sd2, rd2,
):
    ep = lax.axis_index("ep")
    x = lax.axis_index("tp")
    c = ep % 2
    yz = ep // 2
    y = yz // 4
    z = yz % 4
    a1 = z * (1 - c) + y * c
    a2 = y * (1 - c) + z * c
    sib = (ep + 1 - 2 * c, x)
    near = (1, 3, 2)

    def peer(dx, dy, dz):
        return (((y + dy) % 4 * 4 + (z + dz) % 4) * 2 + c, (x + dx) % 4)

    def over_axis1(d):
        return peer(0, d * c, d * (1 - c))

    def over_axis2(d, dx=0):
        return peer(dx, d * (1 - c), d * c)

    def remote(src, dst, ss, rs, dev):
        return pltpu.make_async_remote_copy(
            src_ref=src, dst_ref=dst, send_sem=ss, recv_sem=rs, device_id=dev, device_id_type=MESH
        )

    def sent(ref, sem):
        remote(ref, ref, sem, rb.at[0], sib).wait_send()

    def got(ref, sem):
        remote(ref, ref, sb.at[0], sem, sib).wait_recv()

    def cache_copy(hbm, buf, sem, i):
        return pltpu.make_async_copy(hbm.at[pl.ds(2 * i, 2)], buf.at[pl.ds(2 * i, 2)], sem.at[i])

    smalls = [
        pltpu.make_async_copy(src, dst, small.at[i])
        for i, (src, dst) in enumerate((
            (q_hbm, q_ref), (nk_hbm, nk_ref), (len_hbm, len_ref), (pol_hbm, pol_ref), (ret_hbm, ret_ref),
            (nv_hbm, nv_ref), (routes_hbm, routes_ref), (logit_hbm, logit_ref), (gain_hbm, gain_ref),
        ))
    ]
    cache_copy(k_hbm, kbuf, ksem, 0).start()
    for cp in smalls[:5]:
        cp.start()
    for i in range(1, 4):
        cache_copy(k_hbm, kbuf, ksem, i).start()

    bar = pltpu.get_barrier_semaphore()
    partners = [sib] + [peer(d, 0, 0) for d in near] + [peer(0, d, 0) for d in near] + [peer(0, 0, d) for d in near]
    for dev in partners:
        pl.semaphore_signal(bar, inc=1, device_id=dev, device_id_type=MESH)

    for i in range(4):
        cache_copy(v_hbm, vbuf, vsem, i).start()
    for cp in smalls[5:]:
        cp.start()
    weights = [
        pltpu.make_async_copy(ow_hbm.at[pl.ds(8 * x, 8), 0], owb.at[:, :, pl.ds(0, 128)], wsem.at[0]),
        pltpu.make_async_copy(ow_hbm.at[pl.ds(8 * x, 8), 1], owb.at[:, :, pl.ds(128, 128)], wsem.at[1]),
        pltpu.make_async_copy(res_hbm, resb, wsem.at[2]),
        pltpu.make_async_copy(gate_hbm.at[0], gu.at[0, :, pl.ds(0, 384)], wsem.at[3]),
        pltpu.make_async_copy(up_hbm.at[0], gu.at[0, :, pl.ds(384, 384)], wsem.at[4]),
        pltpu.make_async_copy(gate_hbm.at[1], gu.at[1, :, pl.ds(0, 384)], wsem.at[5]),
        pltpu.make_async_copy(up_hbm.at[1], gu.at[1, :, pl.ds(384, 384)], wsem.at[6]),
        pltpu.make_async_copy(down_hbm, dn, wsem.at[7]),
    ]

    for cp in smalls[:5]:
        cp.wait()

    scale = 128 ** (-0.5)
    pos = lax.broadcasted_iota(jnp.int32, (1, 1024), 1)
    blk = pos >> 6
    for r in range(8):
        length = len_ref[r]
        pol = pol_ref[r]
        used = (length + 63) >> 6
        low = jnp.where(pol == 0, used - 2, jnp.where(pol == 2, 0, used - 1))
        keep = blk >= low
        for k in range(4):
            named = jnp.where(pol == 1, ret_ref[k, r], -1)
            keep = keep | (blk == named)
        bias = jnp.where(keep & (pos < length), 0.0, -jnp.inf).astype(F32)
        qr = q_ref[r]
        own = jnp.sum(qr.astype(F32) * nk_ref[pl.ds(r, 1), :].astype(F32), axis=1, keepdims=True) * scale
        if r % 2 == 0:
            cache_copy(k_hbm, kbuf, ksem, r // 2).wait()
        s = mm(qr, kbuf[r], ((1,), (1,))) * scale + bias
        top = jnp.maximum(jnp.max(s, axis=1, keepdims=True), own)
        p = jnp.exp(s - top)
        ownw = jnp.exp(own - top)
        pbuf[r] = p.astype(BF)
        tbuf[r] = jnp.broadcast_to(jnp.sum(p, axis=1, keepdims=True) + ownw, (16, 128))
        obuf[r] = jnp.broadcast_to(ownw, (16, 128)).astype(BF)
    for w in weights[:3]:
        w.start()
    smalls[5].wait()
    for r in range(8):
        if r % 2 == 0:
            cache_copy(v_hbm, vbuf, vsem, r // 2).wait()
        o = mm(pbuf[r], vbuf[r])
        o = o + obuf[r].astype(F32) * nv_ref[pl.ds(r, 1), :].astype(F32)
        att[:, r, :] = o / tbuf[r]
    for w in weights[3:]:
        w.start()
    here = 4 * a2 + a1
    attg[c, here] = att[...].reshape(128, 128).astype(BF)

    pl.semaphore_wait(bar, len(partners))

    class Gather:
        def __init__(self, buf, sends, gets, sib_sends, sib_gets):
            self.buf, self.sends, self.gets = buf, sends, gets
            self.sib_sends, self.sib_gets = sib_sends, sib_gets

        def row(self, d2, cc):
            base = a2 if cc is c else a1
            return self.buf.at[cc, pl.ds(4 * ((base + 4 - d2) % 4), 4)]

        def send(self, d1, get, dev):
            at = self.buf.at[c, 4 * a2 + (a1 + 4 - d1) % 4]
            remote(at, at, self.sends.at[0], self.gets.at[get], dev).start()

        def over(self, d2):
            at = self.row(d2, c)
            remote(at, at, self.sib_sends.at[0], self.sib_gets.at[d2], sib).start()

        def start(self):
            for d in near:
                self.send(0, 4 + d, over_axis1(d))
            for d in near:
                self.send(0, d, over_axis2(d))

        def relay(self):
            for d1 in near:
                got(self.buf.at[c, 4 * a2 + (a1 + 4 - d1) % 4], self.gets.at[4 + d1])
                for d2 in near:
                    self.send(d1, d2, over_axis2(d2))
            self.over(0)

        def pass_on(self, d2):
            got(self.row(d2, c), self.gets.at[d2])
            self.over(d2)

        def arrived(self, d2):
            got(self.row(d2, 1 - c), self.sib_gets.at[d2])

        def finish(self):
            sent(self.buf.at[c, pl.ds(0, 15)], self.sends.at[0])
            sent(self.buf.at[c], self.sib_sends.at[0])

    attended = Gather(attg, sa, ra, sas, ras)
    attended.start()

    for cp in smalls[6:]:
        cp.wait()
    logits = logit_ref[...]
    grown = jnp.exp(logits - jnp.max(logits, axis=0, keepdims=True))
    rw = grown / jnp.sum(grown, axis=0, keepdims=True)
    sub = lax.broadcasted_iota(jnp.int32, (128, 256), 0)
    mem, wrow = [], []
    for e in range(2):
        hit = routes_ref[...] == ep * 2 + e
        mem.append(jnp.sum(jnp.where(hit, 1.0, 0.0), axis=0, keepdims=True))
        wrow.append(jnp.sum(jnp.where(hit, rw, 0.0), axis=0, keepdims=True))
    memb = jnp.where(sub < 64, mem[0], mem[1])
    tri = jnp.where(
        lax.broadcasted_iota(jnp.int32, (256, 256), 0) < lax.broadcasted_iota(jnp.int32, (256, 256), 1), 1.0, 0.0
    ).astype(BF)
    rank = mm(memb.astype(BF), tri)
    slot = jnp.where(sub < 64, sub, sub - 64).astype(F32)
    chosen = jnp.where(rank == slot, memb, 0.0)
    psel[...] = chosen.astype(BF)
    spread_t = chosen.T
    weight_t = (chosen * jnp.where(sub < 64, wrow[0], wrow[1])).T
    lane = lax.broadcasted_iota(jnp.int32, (256, 128), 1)
    for e in range(2):
        inside = (lane < 64) if e == 0 else (lane >= 64)
        ptb[e] = jnp.where(inside, spread_t, 0.0).astype(BF)
        wcol[e] = jnp.broadcast_to(jnp.sum(jnp.where(inside, weight_t, 0.0), axis=1, keepdims=True), (256, 128))

    attended.relay()
    for d in near:
        attended.pass_on(d)

    weights[0].wait()
    weights[1].wait()

    def project(cc, half):
        total = jnp.zeros((256, 256), F32)
        for g in range(8):
            lhs = attg[cc, :, pl.ds(16 * g, 16), :].reshape(256, 128)
            total = total + mm(lhs, owb[g])
        total = total.reshape(16, 16, 256)
        total = total[:, :8, :128] + total[:, 8:, 128:]
        pb[x, cc] = total.reshape(128, 128).astype(BF)
        for d in near:
            remote(pb.at[x, cc], pb.at[x, cc], sb.at[0], rb.at[2 * d + half], peer(d, 0, 0)).start()

    project(c, 0)
    for d in (0,) + near:
        attended.arrived(d)
    project(1 - c, 1)
    attended.finish()
    weights[2].wait()
    for half, cc in ((0, c), (1, 1 - c)):
        for d in near:
            got(pb.at[(x + 4 - d) % 4, cc], rb.at[2 * d + half])
    for cc in range(2):
        total = pb[0, cc].astype(F32)
        for j in range(1, 4):
            total = total + pb[j, cc].astype(F32)
        total = total.reshape(16, 8, 128)
        for at in range(16):
            nat[at if cc == 0 else at % 4 * 4 + at // 4, cc] = total[at]
    hid[c, here] = (resb[...].astype(F32) + nat[...].reshape(256, 128)).astype(BF)

    hidden = Gather(hid, sc, rc, scs, rcs)
    hidden.start()
    sent(pb.at[pl.ds(0, 3)], sb.at[0])
    block[...] = hid[c, here].astype(F32).T
    hidden.relay()
    for w in weights[3:]:
        w.wait()

    def products(d2, cc, first):
        row = ((a2 if cc is c else a1) + 4 - d2) % 4
        at = [(4 * row + k) * (1 - cc) + (4 * k + row) * cc for k in range(4)]
        picked = mm(psel[...], jnp.concatenate([hid[cc, 4 * row + k] for k in range(4)], axis=1))
        squares = picked * picked
        gain = jnp.concatenate([gain_ref[pl.ds(2 * b + cc, 1), :] for b in at], axis=1)
        squares = squares[:, :128] + squares[:, 128:256] + squares[:, 256:384] + squares[:, 384:]
        lhs = (picked * gain).astype(BF)
        cols = [pl.ds(pl.multiple_of((2 * b + cc) * 128, 128), 128) for b in at]
        for e in range(2):
            rhs = jnp.concatenate([gu[e, col, :] for col in cols], axis=0)
            part = mm(lhs[64 * e : 64 * e + 64], rhs)
            acc[e] = part if first else acc[e] + part
        sq[...] = squares if first else sq[...] + squares

    products(0, c, True)
    waiting = 0
    for d2 in near:
        hidden.pass_on(d2)
        hidden.arrived(waiting)
        products(waiting, 1 - c, False)
        products(d2, c, False)
        waiting = d2
    hidden.arrived(waiting)
    products(waiting, 1 - c, False)
    rs = lax.rsqrt(jnp.sum(sq[...], axis=1, keepdims=True) / 4096 + EPSILON)
    halves = []
    for e in range(2):
        re = rs[64 * e : 64 * e + 64]
        gate = acc[e, :, pl.ds(0, 384)] * re
        up = acc[e, :, pl.ds(384, 384)] * re
        halves.append((gate / (1.0 + jnp.exp(-gate)) * up).astype(BF))
    act = jnp.concatenate(halves, axis=0)
    for e in range(2):
        spread = mm(ptb[e], act)
        aact[:, pl.ds(384 * e, 384)] = (spread * wcol[e][:, :1]).astype(BF)

    def turn(i):
        return jnp.where(i == 0, 2, jnp.where(i == 1, 1, jnp.where(i == 2, 3, 0)))

    def dest(n, cc):
        d1 = jnp.where(n < 12, turn(n % 3), 0)
        d2 = turn(jnp.where(n < 12, n // 3, n - 12))
        dy = d1 * (1 - cc) + d2 * cc
        dz = d2 * (1 - cc) + d1 * cc
        return d1, d2, (y + dy) % 4 * 4 + (z + dz) % 4

    def down(n):
        mine_col = pl.multiple_of((2 * dest(n, c)[2] + c) * 128, 128)
        sib_col = pl.multiple_of((2 * dest(n, 1 - c)[2] + 1 - c) * 128, 128)
        rhs = jnp.concatenate([dn[:, pl.ds(sib_col, 128)], dn[:, pl.ds(mine_col, 128)]], axis=1)
        both = mm(aact[...], rhs)
        psib[n] = both[:, :128].astype(BF)
        remote(psib.at[n], srec.at[n], sds.at[0], rds.at[n], sib).start()
        pown[n] = both[:, 128:]

    def join(n):
        got(srec.at[n], rds.at[n])
        return pown[n] + srec[n].astype(F32)

    def forward(n):
        d1, d2, _ = dest(n, c)
        qbuf[n] = join(n).astype(BF)
        remote(qbuf.at[n], r1.at[d2, n % 3], sd1.at[0], rd1.at[d2], peer(0, d1 * (1 - c), d1 * c)).start()

    down(0)

    def step(n, _):
        down(n)
        forward(n - 1)
        return 0

    lax.fori_loop(1, 13, step, 0)
    for n in range(13, 16):
        down(n)
    hidden.finish()

    def slab(j):
        return pl.ds(pl.multiple_of(32 * (j % 4), 32), 32)

    for i2, d2 in enumerate((2, 1, 3, 0)):
        total = join(12 + i2)
        got(r1.at[d2], rd1.at[d2])
        for i1 in range(3):
            total = total + r1[d2, i1].astype(F32)
        turned = total.T
        tb[d2] = turned.astype(BF)
        if d2 == 0:
            last[...] = block[slab(x), :] + jnp.where(x == 0, turned[:32], jnp.where(x == 1, turned[32:64], jnp.where(x == 2, turned[64:96], turned[96:])))
        for dx in (2, 1, 3, 0):
            if d2 or dx:
                dev = peer(dx, d2 * c, d2 * (1 - c))
                remote(tb.at[d2, slab(x + dx)], r2.at[4 * d2 + dx], sd2.at[0], rd2.at[0], dev).start()
    sent(psib, sds.at[0])
    sent(qbuf, sd1.at[0])
    got(r2.at[pl.ds(1, 15)], rd2.at[0])
    total = last[...]
    for k in range(1, 16):
        total = total + r2[k].astype(F32)
    out_ref[...] = total.astype(BF)
    sent(r2.at[pl.ds(1, 15)], sd2.at[0])


def per_device(
    queries, key_cache, stored_value_cache, new_key, incoming_value, lengths, policy, retained_blocks,
    out_weight, residual, norm_gain, routes, router_logits, gate_weight, up_weight, down_weight,
):
    vm = pl.BlockSpec(memory_space=pltpu.VMEM)
    hb = pl.BlockSpec(memory_space=pl.ANY)
    dma = pltpu.SemaphoreType.DMA
    scratch = [
        pltpu.SMEM((8,), jnp.int32),
        pltpu.SMEM((8,), jnp.int32),
        pltpu.SMEM((4, 8), jnp.int32),
        pltpu.VMEM((8, 16, 128), BF),
        pltpu.VMEM((8, 128), BF),
        pltpu.VMEM((8, 128), BF),
        pltpu.VMEM((8, 256), jnp.int32),
        pltpu.VMEM((8, 256), F32),
        pltpu.VMEM((32, 128), F32),
        pltpu.VMEM((8, 1024, 128), BF),
        pltpu.VMEM((8, 1024, 128), BF),
        pltpu.VMEM((8, 16, 1024), BF),
        pltpu.VMEM((8, 16, 128), F32),
        pltpu.VMEM((8, 16, 128), BF),
        pltpu.VMEM((16, 8, 128), F32),
        pltpu.VMEM((2, 16, 128, 128), BF),
        pltpu.VMEM((8, 128, 256), BF),
        pltpu.VMEM((4, 2, 128, 128), BF),
        pltpu.VMEM((16, 2, 8, 128), F32),
        pltpu.VMEM((256, 128), BF),
        pltpu.VMEM((2, 16, 256, 128), BF),
        pltpu.VMEM((128, 128), F32),
        pltpu.VMEM((2, 4096, 768), BF),
        pltpu.VMEM((768, 4096), BF),
        pltpu.VMEM((2, 256, 128), BF),
        pltpu.VMEM((128, 256), BF),
        pltpu.VMEM((2, 256, 128), F32),
        pltpu.VMEM((2, 64, 768), F32),
        pltpu.VMEM((256, 768), BF),
        pltpu.VMEM((16, 256, 128), BF),
        pltpu.VMEM((16, 256, 128), F32),
        pltpu.VMEM((16, 256, 128), BF),
        pltpu.VMEM((12, 256, 128), BF),
        pltpu.VMEM((4, 3, 256, 128), BF),
        pltpu.VMEM((4, 128, 256), BF),
        pltpu.VMEM((32, 256), F32),
        pltpu.VMEM((128, 256), F32),
        pltpu.VMEM((16, 32, 256), BF),
        dma((9,)), dma((4,)), dma((4,)), dma((8,)),
        dma((1,)), dma((8,)), dma((1,)), dma((4,)),
        dma((1,)), dma((8,)),
        dma((1,)), dma((8,)), dma((1,)), dma((4,)),
        dma((1,)), dma((16,)), dma((1,)), dma((4,)),
        dma((1,)), dma((1,)),
    ]
    return pl.pallas_call(
        kernel,
        out_shape=jax.ShapeDtypeStruct((32, 256), BF),
        in_specs=[hb] * 16,
        out_specs=vm,
        scratch_shapes=scratch,
        name="decode_step",
        cost_estimate=pl.CostEstimate(flops=3_000_000_000, bytes_accessed=26_000_000, transcendentals=200_000),
        compiler_params=pltpu.CompilerParams(
            collective_id=0, has_side_effects=True, vmem_limit_bytes=56 * 2**20
        ),
    )(
        lengths, policy.reshape(8), retained_blocks.transpose(1, 2, 0).reshape(4, 8),
        queries, new_key.reshape(8, 128), incoming_value.reshape(8, 128),
        routes.T, router_logits.T, norm_gain.reshape(32, 128),
        key_cache.reshape(8, 1024, 128), stored_value_cache.reshape(8, 1024, 128),
        out_weight.reshape(32, 2, 128, 128), residual,
        gate_weight, up_weight, down_weight.reshape(768, 4096),
    ).T


def solution(mesh):
    return jax.shard_map(
        per_device,
        mesh=mesh,
        in_specs=(
            P("ep", "tp", None),
            P("ep", "tp", None, None),
            P("ep", "tp", None, None),
            P("ep", "tp", None),
            P("ep", "tp", None),
            P("ep"),
            P("ep", "tp"),
            P("ep", "tp", None),
            P(None, "ep"),
            P(None, "ep"),
            P(),
            P(),
            P(),
            P("ep", None, "tp"),
            P("ep", None, "tp"),
            P("ep", "tp", None),
        ),
        out_specs=P(None, ("ep", "tp")),
        check_vma=False,
    )
```

```python
import functools
import jax
import jax.numpy as jnp
from jax import lax
from jax.sharding import PartitionSpec as P
from jax.experimental import pallas as pl
from jax.experimental.pallas import tpu as pltpu

TOPK = 8
CAP = 64
EPSILON = 1e-06
LAG = 4
MESH = pl.DeviceIdType.MESH
BF = jnp.bfloat16
F32 = jnp.float32


def mm(a, b, dims=((1,), (0,))):
    return lax.dot_general(a, b, (dims, ((), ())), preferred_element_type=F32)


def kernel(
    len_hbm, pol_hbm, ret_hbm, q_hbm, nk_hbm, nv_hbm, routes_hbm, logit_hbm, gain_hbm,
    k_hbm, v_hbm, ow_hbm, res_hbm, gate_hbm, up_hbm, down_hbm,
    out_ref,
    len_ref, pol_ref, ret_ref, q_ref, nk_ref, nv_ref, routes_ref, logit_ref, gain_ref,
    kbuf, vbuf, pbuf, tbuf, obuf, att, attg, owb, pb, nat, resb,
    hid, sq, gu, dn, ptb, psel, wcol, acc, aact,
    psib, pown, srec, qbuf, r1, tb, last, block, r2,
    small, ksem, vsem, wsem,
    sa, ra, sas, ras, sb, rb, sc, rc, scs, rcs, sds, rds, sd1, rd1, sd2, rd2,
):
    ep = lax.axis_index("ep")
    x = lax.axis_index("tp")
    c = ep % 2
    yz = ep // 2
    y = yz // 4
    z = yz % 4
    a1 = z * (1 - c) + y * c
    a2 = y * (1 - c) + z * c
    sib = (ep + 1 - 2 * c, x)
    near = (1, 3, 2)

    def peer(dx, dy, dz):
        return (((y + dy) % 4 * 4 + (z + dz) % 4) * 2 + c, (x + dx) % 4)

    def over_axis1(d):
        return peer(0, d * c, d * (1 - c))

    def over_axis2(d, dx=0):
        return peer(dx, d * (1 - c), d * c)

    def remote(src, dst, ss, rs, dev):
        return pltpu.make_async_remote_copy(
            src_ref=src, dst_ref=dst, send_sem=ss, recv_sem=rs, device_id=dev, device_id_type=MESH
        )

    def sent(ref, sem):
        remote(ref, ref, sem, rb.at[0], sib).wait_send()

    def got(ref, sem):
        remote(ref, ref, sb.at[0], sem, sib).wait_recv()

    def cache_copy(hbm, buf, sem, i):
        return pltpu.make_async_copy(hbm.at[pl.ds(2 * i, 2)], buf.at[pl.ds(2 * i, 2)], sem.at[i])

    smalls = [
        pltpu.make_async_copy(src, dst, small.at[i])
        for i, (src, dst) in enumerate((
            (q_hbm, q_ref), (nk_hbm, nk_ref), (len_hbm, len_ref), (pol_hbm, pol_ref), (ret_hbm, ret_ref),
            (nv_hbm, nv_ref), (routes_hbm, routes_ref), (logit_hbm, logit_ref), (gain_hbm, gain_ref),
        ))
    ]
    cache_copy(k_hbm, kbuf, ksem, 0).start()
    for cp in smalls[:5]:
        cp.start()
    for i in range(1, 4):
        cache_copy(k_hbm, kbuf, ksem, i).start()

    bar = pltpu.get_barrier_semaphore()
    partners = [sib] + [peer(d, 0, 0) for d in near] + [peer(0, d, 0) for d in near] + [peer(0, 0, d) for d in near]
    for dev in partners:
        pl.semaphore_signal(bar, inc=1, device_id=dev, device_id_type=MESH)

    for i in range(4):
        cache_copy(v_hbm, vbuf, vsem, i).start()
    for cp in smalls[5:]:
        cp.start()
    weights = [
        pltpu.make_async_copy(ow_hbm.at[pl.ds(8 * x, 8), 0], owb.at[:, :, pl.ds(0, 128)], wsem.at[0]),
        pltpu.make_async_copy(ow_hbm.at[pl.ds(8 * x, 8), 1], owb.at[:, :, pl.ds(128, 128)], wsem.at[1]),
        pltpu.make_async_copy(res_hbm, resb, wsem.at[2]),
        pltpu.make_async_copy(gate_hbm.at[0], gu.at[0, :, pl.ds(0, 384)], wsem.at[3]),
        pltpu.make_async_copy(up_hbm.at[0], gu.at[0, :, pl.ds(384, 384)], wsem.at[4]),
        pltpu.make_async_copy(gate_hbm.at[1], gu.at[1, :, pl.ds(0, 384)], wsem.at[5]),
        pltpu.make_async_copy(up_hbm.at[1], gu.at[1, :, pl.ds(384, 384)], wsem.at[6]),
        pltpu.make_async_copy(down_hbm, dn, wsem.at[7]),
    ]

    for cp in smalls[:5]:
        cp.wait()

    scale = 128 ** (-0.5)
    pos = lax.broadcasted_iota(jnp.int32, (1, 1024), 1)
    blk = pos >> 6
    for r in range(8):
        length = len_ref[r]
        pol = pol_ref[r]
        used = (length + 63) >> 6
        low = jnp.where(pol == 0, used - 2, jnp.where(pol == 2, 0, used - 1))
        keep = blk >= low
        for k in range(4):
            named = jnp.where(pol == 1, ret_ref[k, r], -1)
            keep = keep | (blk == named)
        bias = jnp.where(keep & (pos < length), 0.0, -jnp.inf).astype(F32)
        qr = q_ref[r]
        own = jnp.sum(qr.astype(F32) * nk_ref[pl.ds(r, 1), :].astype(F32), axis=1, keepdims=True) * scale
        if r % 2 == 0:
            cache_copy(k_hbm, kbuf, ksem, r // 2).wait()
        s = mm(qr, kbuf[r], ((1,), (1,))) * scale + bias
        top = jnp.maximum(jnp.max(s, axis=1, keepdims=True), own)
        p = jnp.exp(s - top)
        ownw = jnp.exp(own - top)
        pbuf[r] = p.astype(BF)
        tbuf[r] = jnp.broadcast_to(jnp.sum(p, axis=1, keepdims=True) + ownw, (16, 128))
        obuf[r] = jnp.broadcast_to(ownw, (16, 128)).astype(BF)
    for w in weights[:3]:
        w.start()
    smalls[5].wait()
    for r in range(8):
        if r % 2 == 0:
            cache_copy(v_hbm, vbuf, vsem, r // 2).wait()
        o = mm(pbuf[r], vbuf[r])
        o = o + obuf[r].astype(F32) * nv_ref[pl.ds(r, 1), :].astype(F32)
        att[:, r, :] = o / tbuf[r]
    for w in weights[3:]:
        w.start()
    here = 4 * a2 + a1
    attg[c, here] = att[...].reshape(128, 128).astype(BF)

    pl.semaphore_wait(bar, len(partners))

    class Gather:
        def __init__(self, buf, sends, gets, sib_sends, sib_gets):
            self.buf, self.sends, self.gets = buf, sends, gets
            self.sib_sends, self.sib_gets = sib_sends, sib_gets

        def row(self, d2, cc):
            base = a2 if cc is c else a1
            return self.buf.at[cc, pl.ds(4 * ((base + 4 - d2) % 4), 4)]

        def send(self, d1, get, dev):
            at = self.buf.at[c, 4 * a2 + (a1 + 4 - d1) % 4]
            remote(at, at, self.sends.at[0], self.gets.at[get], dev).start()

        def over(self, d2):
            at = self.row(d2, c)
            remote(at, at, self.sib_sends.at[0], self.sib_gets.at[d2], sib).start()

        def start(self):
            for d in near:
                self.send(0, 4 + d, over_axis1(d))
            for d in near:
                self.send(0, d, over_axis2(d))

        def relay(self):
            for d1 in near:
                got(self.buf.at[c, 4 * a2 + (a1 + 4 - d1) % 4], self.gets.at[4 + d1])
                for d2 in near:
                    self.send(d1, d2, over_axis2(d2))
            self.over(0)

        def pass_on(self, d2):
            got(self.row(d2, c), self.gets.at[d2])
            self.over(d2)

        def arrived(self, d2):
            got(self.row(d2, 1 - c), self.sib_gets.at[d2])

        def finish(self):
            sent(self.buf.at[c, pl.ds(0, 15)], self.sends.at[0])
            sent(self.buf.at[c], self.sib_sends.at[0])

    attended = Gather(attg, sa, ra, sas, ras)
    attended.start()

    for cp in smalls[6:]:
        cp.wait()
    logits = logit_ref[...]
    grown = jnp.exp(logits - jnp.max(logits, axis=0, keepdims=True))
    rw = grown / jnp.sum(grown, axis=0, keepdims=True)
    sub = lax.broadcasted_iota(jnp.int32, (128, 256), 0)
    mem, wrow = [], []
    for e in range(2):
        hit = routes_ref[...] == ep * 2 + e
        mem.append(jnp.sum(jnp.where(hit, 1.0, 0.0), axis=0, keepdims=True))
        wrow.append(jnp.sum(jnp.where(hit, rw, 0.0), axis=0, keepdims=True))
    memb = jnp.where(sub < 64, mem[0], mem[1])
    tri = jnp.where(
        lax.broadcasted_iota(jnp.int32, (256, 256), 0) < lax.broadcasted_iota(jnp.int32, (256, 256), 1), 1.0, 0.0
    ).astype(BF)
    rank = mm(memb.astype(BF), tri)
    slot = jnp.where(sub < 64, sub, sub - 64).astype(F32)
    chosen = jnp.where(rank == slot, memb, 0.0)
    psel[...] = chosen.astype(BF)
    spread_t = chosen.T
    weight_t = (chosen * jnp.where(sub < 64, wrow[0], wrow[1])).T
    lane = lax.broadcasted_iota(jnp.int32, (256, 128), 1)
    for e in range(2):
        inside = (lane < 64) if e == 0 else (lane >= 64)
        ptb[e] = jnp.where(inside, spread_t, 0.0).astype(BF)
        wcol[e] = jnp.broadcast_to(jnp.sum(jnp.where(inside, weight_t, 0.0), axis=1, keepdims=True), (256, 128))

    attended.relay()
    for d in near:
        attended.pass_on(d)

    weights[0].wait()
    weights[1].wait()

    def project(cc, half):
        total = jnp.zeros((256, 256), F32)
        for g in range(8):
            lhs = attg[cc, :, pl.ds(16 * g, 16), :].reshape(256, 128)
            total = total + mm(lhs, owb[g])
        total = total.reshape(16, 16, 256)
        total = total[:, :8, :128] + total[:, 8:, 128:]
        pb[x, cc] = total.reshape(128, 128).astype(BF)
        for d in near:
            remote(pb.at[x, cc], pb.at[x, cc], sb.at[0], rb.at[2 * d + half], peer(d, 0, 0)).start()

    project(c, 0)
    for d in (0,) + near:
        attended.arrived(d)
    project(1 - c, 1)
    attended.finish()
    weights[2].wait()
    for half, cc in ((0, c), (1, 1 - c)):
        for d in near:
            got(pb.at[(x + 4 - d) % 4, cc], rb.at[2 * d + half])
    for cc in range(2):
        total = pb[0, cc].astype(F32)
        for j in range(1, 4):
            total = total + pb[j, cc].astype(F32)
        total = total.reshape(16, 8, 128)
        for at in range(16):
            nat[at if cc == 0 else at % 4 * 4 + at // 4, cc] = total[at]
    hid[c, here] = (resb[...].astype(F32) + nat[...].reshape(256, 128)).astype(BF)

    hidden = Gather(hid, sc, rc, scs, rcs)
    hidden.start()
    sent(pb.at[pl.ds(0, 3)], sb.at[0])
    block[...] = hid[c, here].astype(F32).T
    hidden.relay()
    for w in weights[3:]:
        w.wait()

    def products(d2, cc, first):
        row = ((a2 if cc is c else a1) + 4 - d2) % 4
        at = [(4 * row + k) * (1 - cc) + (4 * k + row) * cc for k in range(4)]
        picked = mm(psel[...], jnp.concatenate([hid[cc, 4 * row + k] for k in range(4)], axis=1))
        squares = picked * picked
        gain = jnp.concatenate([gain_ref[pl.ds(2 * b + cc, 1), :] for b in at], axis=1)
        squares = squares[:, :128] + squares[:, 128:256] + squares[:, 256:384] + squares[:, 384:]
        lhs = (picked * gain).astype(BF)
        cols = [pl.ds(pl.multiple_of((2 * b + cc) * 128, 128), 128) for b in at]
        for e in range(2):
            rhs = jnp.concatenate([gu[e, col, :] for col in cols], axis=0)
            part = mm(lhs[64 * e : 64 * e + 64], rhs)
            acc[e] = part if first else acc[e] + part
        sq[...] = squares if first else sq[...] + squares

    products(0, c, True)
    waiting = 0
    for d2 in near:
        hidden.pass_on(d2)
        hidden.arrived(waiting)
        products(waiting, 1 - c, False)
        products(d2, c, False)
        waiting = d2
    hidden.arrived(waiting)
    products(waiting, 1 - c, False)
    rs = lax.rsqrt(jnp.sum(sq[...], axis=1, keepdims=True) / 4096 + EPSILON)
    halves = []
    for e in range(2):
        re = rs[64 * e : 64 * e + 64]
        gate = acc[e, :, pl.ds(0, 384)] * re
        up = acc[e, :, pl.ds(384, 384)] * re
        halves.append((gate / (1.0 + jnp.exp(-gate)) * up).astype(BF))
    act = jnp.concatenate(halves, axis=0)
    for e in range(2):
        spread = mm(ptb[e], act)
        aact[:, pl.ds(384 * e, 384)] = (spread * wcol[e][:, :1]).astype(BF)

    def turn(i):
        return jnp.where(i == 0, 2, jnp.where(i == 1, 1, jnp.where(i == 2, 3, 0)))

    def dest(n, cc):
        d1 = jnp.where(n < 12, turn(n % 3), 0)
        d2 = turn(jnp.where(n < 12, n // 3, n - 12))
        dy = d1 * (1 - cc) + d2 * cc
        dz = d2 * (1 - cc) + d1 * cc
        return d1, d2, (y + dy) % 4 * 4 + (z + dz) % 4

    def down(n):
        mine_col = pl.multiple_of((2 * dest(n, c)[2] + c) * 128, 128)
        sib_col = pl.multiple_of((2 * dest(n, 1 - c)[2] + 1 - c) * 128, 128)
        rhs = jnp.concatenate([dn[:, pl.ds(sib_col, 128)], dn[:, pl.ds(mine_col, 128)]], axis=1)
        both = mm(aact[...], rhs)
        psib[n] = both[:, :128].astype(BF)
        remote(psib.at[n], srec.at[n], sds.at[0], rds.at[n], sib).start()
        pown[n] = both[:, 128:]

    def join(n):
        got(srec.at[n], rds.at[n])
        return pown[n] + srec[n].astype(F32)

    def forward(n):
        d1, d2, _ = dest(n, c)
        qbuf[n] = join(n).astype(BF)
        remote(qbuf.at[n], r1.at[d2, n % 3], sd1.at[0], rd1.at[d2], peer(0, d1 * (1 - c), d1 * c)).start()

    for n in range(LAG):
        down(n)

    def step(n, _):
        down(n)
        forward(n - LAG)
        return 0

    lax.fori_loop(LAG, 12 + LAG, step, 0)
    for n in range(12 + LAG, 16):
        down(n)
    hidden.finish()

    def slab(j):
        return pl.ds(pl.multiple_of(32 * (j % 4), 32), 32)

    for i2, d2 in enumerate((2, 1, 3, 0)):
        total = join(12 + i2)
        got(r1.at[d2], rd1.at[d2])
        for i1 in range(3):
            total = total + r1[d2, i1].astype(F32)
        turned = total.T
        tb[d2] = turned.astype(BF)
        if d2 == 0:
            last[...] = block[slab(x), :] + jnp.where(x == 0, turned[:32], jnp.where(x == 1, turned[32:64], jnp.where(x == 2, turned[64:96], turned[96:])))
        for dx in (2, 1, 3, 0):
            if d2 or dx:
                dev = peer(dx, d2 * c, d2 * (1 - c))
                remote(tb.at[d2, slab(x + dx)], r2.at[4 * d2 + dx], sd2.at[0], rd2.at[0], dev).start()
    sent(psib, sds.at[0])
    sent(qbuf, sd1.at[0])
    got(r2.at[pl.ds(1, 15)], rd2.at[0])
    total = last[...]
    for k in range(1, 16):
        total = total + r2[k].astype(F32)
    out_ref[...] = total.astype(BF)
    sent(r2.at[pl.ds(1, 15)], sd2.at[0])


def per_device(
    queries, key_cache, stored_value_cache, new_key, incoming_value, lengths, policy, retained_blocks,
    out_weight, residual, norm_gain, routes, router_logits, gate_weight, up_weight, down_weight,
):
    vm = pl.BlockSpec(memory_space=pltpu.VMEM)
    hb = pl.BlockSpec(memory_space=pl.ANY)
    dma = pltpu.SemaphoreType.DMA
    scratch = [
        pltpu.SMEM((8,), jnp.int32),
        pltpu.SMEM((8,), jnp.int32),
        pltpu.SMEM((4, 8), jnp.int32),
        pltpu.VMEM((8, 16, 128), BF),
        pltpu.VMEM((8, 128), BF),
        pltpu.VMEM((8, 128), BF),
        pltpu.VMEM((8, 256), jnp.int32),
        pltpu.VMEM((8, 256), F32),
        pltpu.VMEM((32, 128), F32),
        pltpu.VMEM((8, 1024, 128), BF),
        pltpu.VMEM((8, 1024, 128), BF),
        pltpu.VMEM((8, 16, 1024), BF),
        pltpu.VMEM((8, 16, 128), F32),
        pltpu.VMEM((8, 16, 128), BF),
        pltpu.VMEM((16, 8, 128), F32),
        pltpu.VMEM((2, 16, 128, 128), BF),
        pltpu.VMEM((8, 128, 256), BF),
        pltpu.VMEM((4, 2, 128, 128), BF),
        pltpu.VMEM((16, 2, 8, 128), F32),
        pltpu.VMEM((256, 128), BF),
        pltpu.VMEM((2, 16, 256, 128), BF),
        pltpu.VMEM((128, 128), F32),
        pltpu.VMEM((2, 4096, 768), BF),
        pltpu.VMEM((768, 4096), BF),
        pltpu.VMEM((2, 256, 128), BF),
        pltpu.VMEM((128, 256), BF),
        pltpu.VMEM((2, 256, 128), F32),
        pltpu.VMEM((2, 64, 768), F32),
        pltpu.VMEM((256, 768), BF),
        pltpu.VMEM((16, 256, 128), BF),
        pltpu.VMEM((16, 256, 128), F32),
        pltpu.VMEM((16, 256, 128), BF),
        pltpu.VMEM((12, 256, 128), BF),
        pltpu.VMEM((4, 3, 256, 128), BF),
        pltpu.VMEM((4, 128, 256), BF),
        pltpu.VMEM((32, 256), F32),
        pltpu.VMEM((128, 256), F32),
        pltpu.VMEM((16, 32, 256), BF),
        dma((9,)), dma((4,)), dma((4,)), dma((8,)),
        dma((1,)), dma((8,)), dma((1,)), dma((4,)),
        dma((1,)), dma((8,)),
        dma((1,)), dma((8,)), dma((1,)), dma((4,)),
        dma((1,)), dma((16,)), dma((1,)), dma((4,)),
        dma((1,)), dma((1,)),
    ]
    return pl.pallas_call(
        kernel,
        out_shape=jax.ShapeDtypeStruct((32, 256), BF),
        in_specs=[hb] * 16,
        out_specs=vm,
        scratch_shapes=scratch,
        name="decode_step",
        cost_estimate=pl.CostEstimate(flops=3_000_000_000, bytes_accessed=26_000_000, transcendentals=200_000),
        compiler_params=pltpu.CompilerParams(
            collective_id=0, has_side_effects=True, vmem_limit_bytes=56 * 2**20
        ),
    )(
        lengths, policy.reshape(8), retained_blocks.transpose(1, 2, 0).reshape(4, 8),
        queries, new_key.reshape(8, 128), incoming_value.reshape(8, 128),
        routes.T, router_logits.T, norm_gain.reshape(32, 128),
        key_cache.reshape(8, 1024, 128), stored_value_cache.reshape(8, 1024, 128),
        out_weight.reshape(32, 2, 128, 128), residual,
        gate_weight, up_weight, down_weight.reshape(768, 4096),
    ).T


def solution(mesh):
    return jax.shard_map(
        per_device,
        mesh=mesh,
        in_specs=(
            P("ep", "tp", None),
            P("ep", "tp", None, None),
            P("ep", "tp", None, None),
            P("ep", "tp", None),
            P("ep", "tp", None),
            P("ep"),
            P("ep", "tp"),
            P("ep", "tp", None),
            P(None, "ep"),
            P(None, "ep"),
            P(),
            P(),
            P(),
            P("ep", None, "tp"),
            P("ep", None, "tp"),
            P("ep", "tp", None),
        ),
        out_specs=P(None, ("ep", "tp")),
        check_vma=False,
    )
```

```python
import functools
import jax
import jax.numpy as jnp
from jax import lax
from jax.sharding import PartitionSpec as P
from jax.experimental import pallas as pl
from jax.experimental.pallas import tpu as pltpu

TOPK = 8
CAP = 64
EPSILON = 1e-06
LAG = 4
MESH = pl.DeviceIdType.MESH
BF = jnp.bfloat16
F32 = jnp.float32


def mm(a, b, dims=((1,), (0,))):
    return lax.dot_general(a, b, (dims, ((), ())), preferred_element_type=F32)


def kernel(
    len_hbm, pol_hbm, ret_hbm, q_hbm, nk_hbm, nv_hbm, routes_hbm, logit_hbm, gain_hbm,
    k_hbm, v_hbm, ow_hbm, res_hbm, gate_hbm, up_hbm, down_hbm,
    out_ref,
    len_ref, pol_ref, ret_ref, q_ref, nk_ref, nv_ref, routes_ref, logit_ref, gain_ref,
    kbuf, vbuf, pbuf, tbuf, obuf, att, attg, owb, pb, nat, resb,
    hid, sq, gu, dn, ptb, psel, wcol, acc, aact,
    psib, pown, srec, qbuf, r1, tb, last, block, r2,
    small, ksem, vsem, wsem,
    sa, ra, sas, ras, sb, rb, sc, rc, scs, rcs, sds, rds, sd1, rd1, sd2, rd2,
):
    ep = lax.axis_index("ep")
    x = lax.axis_index("tp")
    c = ep % 2
    yz = ep // 2
    y = yz // 4
    z = yz % 4
    a1 = z * (1 - c) + y * c
    a2 = y * (1 - c) + z * c
    sib = (ep + 1 - 2 * c, x)
    near = (1, 3, 2)

    def peer(dx, dy, dz):
        return (((y + dy) % 4 * 4 + (z + dz) % 4) * 2 + c, (x + dx) % 4)

    def over_axis1(d):
        return peer(0, d * c, d * (1 - c))

    def over_axis2(d, dx=0):
        return peer(dx, d * (1 - c), d * c)

    def remote(src, dst, ss, rs, dev):
        return pltpu.make_async_remote_copy(
            src_ref=src, dst_ref=dst, send_sem=ss, recv_sem=rs, device_id=dev, device_id_type=MESH
        )

    def sent(ref, sem):
        remote(ref, ref, sem, rb.at[0], sib).wait_send()

    def got(ref, sem):
        remote(ref, ref, sb.at[0], sem, sib).wait_recv()

    def cache_copy(hbm, buf, sem, i):
        return pltpu.make_async_copy(hbm.at[pl.ds(2 * i, 2)], buf.at[pl.ds(2 * i, 2)], sem.at[i])

    smalls = [
        pltpu.make_async_copy(src, dst, small.at[i])
        for i, (src, dst) in enumerate((
            (q_hbm, q_ref), (nk_hbm, nk_ref), (len_hbm, len_ref), (pol_hbm, pol_ref), (ret_hbm, ret_ref),
            (nv_hbm, nv_ref), (routes_hbm, routes_ref), (logit_hbm, logit_ref), (gain_hbm, gain_ref),
        ))
    ]
    cache_copy(k_hbm, kbuf, ksem, 0).start()
    for cp in smalls[:5]:
        cp.start()
    for i in range(1, 4):
        cache_copy(k_hbm, kbuf, ksem, i).start()

    bar = pltpu.get_barrier_semaphore()
    partners = [sib] + [peer(d, 0, 0) for d in near] + [peer(0, d, 0) for d in near] + [peer(0, 0, d) for d in near]
    for dev in partners:
        pl.semaphore_signal(bar, inc=1, device_id=dev, device_id_type=MESH)

    for i in range(4):
        cache_copy(v_hbm, vbuf, vsem, i).start()
    for cp in smalls[5:]:
        cp.start()
    weights = [
        pltpu.make_async_copy(ow_hbm.at[pl.ds(8 * x, 8), 0], owb.at[:, :, pl.ds(0, 128)], wsem.at[0]),
        pltpu.make_async_copy(ow_hbm.at[pl.ds(8 * x, 8), 1], owb.at[:, :, pl.ds(128, 128)], wsem.at[1]),
        pltpu.make_async_copy(res_hbm, resb, wsem.at[2]),
        pltpu.make_async_copy(gate_hbm.at[0], gu.at[0, :, pl.ds(0, 384)], wsem.at[3]),
        pltpu.make_async_copy(up_hbm.at[0], gu.at[0, :, pl.ds(384, 384)], wsem.at[4]),
        pltpu.make_async_copy(gate_hbm.at[1], gu.at[1, :, pl.ds(0, 384)], wsem.at[5]),
        pltpu.make_async_copy(up_hbm.at[1], gu.at[1, :, pl.ds(384, 384)], wsem.at[6]),
        pltpu.make_async_copy(down_hbm, dn, wsem.at[7]),
    ]

    for cp in smalls[:5]:
        cp.wait()

    scale = 128 ** (-0.5)
    pos = lax.broadcasted_iota(jnp.int32, (1, 1024), 1)
    blk = pos >> 6
    for r in range(8):
        length = len_ref[r]
        pol = pol_ref[r]
        used = (length + 63) >> 6
        low = jnp.where(pol == 0, used - 2, jnp.where(pol == 2, 0, used - 1))
        keep = blk >= low
        for k in range(4):
            named = jnp.where(pol == 1, ret_ref[k, r], -1)
            keep = keep | (blk == named)
        bias = jnp.where(keep & (pos < length), 0.0, -jnp.inf).astype(F32)
        qr = q_ref[r]
        own = jnp.sum(qr.astype(F32) * nk_ref[pl.ds(r, 1), :].astype(F32), axis=1, keepdims=True) * scale
        if r % 2 == 0:
            cache_copy(k_hbm, kbuf, ksem, r // 2).wait()
        s = mm(qr, kbuf[r], ((1,), (1,))) * scale + bias
        top = jnp.maximum(jnp.max(s, axis=1, keepdims=True), own)
        p = jnp.exp(s - top)
        ownw = jnp.exp(own - top)
        pbuf[r] = p.astype(BF)
        tbuf[r] = jnp.broadcast_to(jnp.sum(p, axis=1, keepdims=True) + ownw, (16, 128))
        obuf[r] = jnp.broadcast_to(ownw, (16, 128)).astype(BF)
    for w in weights[:3]:
        w.start()
    smalls[5].wait()
    for r in range(8):
        if r % 2 == 0:
            cache_copy(v_hbm, vbuf, vsem, r // 2).wait()
        o = mm(pbuf[r], vbuf[r])
        o = o + obuf[r].astype(F32) * nv_ref[pl.ds(r, 1), :].astype(F32)
        att[:, r, :] = o / tbuf[r]
    for w in weights[3:]:
        w.start()
    here = 4 * a2 + a1
    attg[c, here] = att[...].reshape(128, 128).astype(BF)

    pl.semaphore_wait(bar, len(partners))

    class Gather:
        def __init__(self, buf, sends, gets, sib_sends, sib_gets):
            self.buf, self.sends, self.gets = buf, sends, gets
            self.sib_sends, self.sib_gets = sib_sends, sib_gets

        def row(self, d2, cc):
            base = a2 if cc is c else a1
            return self.buf.at[cc, pl.ds(4 * ((base + 4 - d2) % 4), 4)]

        def send(self, d1, get, dev):
            at = self.buf.at[c, 4 * a2 + (a1 + 4 - d1) % 4]
            remote(at, at, self.sends.at[0], self.gets.at[get], dev).start()

        def over(self, d2):
            at = self.row(d2, c)
            remote(at, at, self.sib_sends.at[0], self.sib_gets.at[d2], sib).start()

        def start(self):
            for d in near:
                self.send(0, 4 + d, over_axis1(d))
            for d in near:
                self.send(0, d if d != 2 else 8, over_axis2(d))

        def relay(self):
            for d1 in near:
                got(self.buf.at[c, 4 * a2 + (a1 + 4 - d1) % 4], self.gets.at[4 + d1])
                for d2 in near:
                    self.send(d1, d2 if d2 != 2 else 8 + d1, over_axis2(d2))
            self.over(0)

        def pass_on(self, d2):
            if d2 != 2:
                got(self.row(d2, c), self.gets.at[d2])
                self.over(d2)
                return
            for d1 in (0,) + near:
                at = self.buf.at[c, 4 * ((a2 + 2) % 4) + (a1 + 4 - d1) % 4]
                got(at, self.gets.at[8 + d1])
                remote(at, at, self.sib_sends.at[0], self.sib_gets.at[d2], sib).start()

        def arrived(self, d2):
            got(self.row(d2, 1 - c), self.sib_gets.at[d2])

        def finish(self):
            sent(self.buf.at[c, pl.ds(0, 15)], self.sends.at[0])
            sent(self.buf.at[c], self.sib_sends.at[0])

    attended = Gather(attg, sa, ra, sas, ras)
    attended.start()

    for cp in smalls[6:]:
        cp.wait()
    logits = logit_ref[...]
    grown = jnp.exp(logits - jnp.max(logits, axis=0, keepdims=True))
    rw = grown / jnp.sum(grown, axis=0, keepdims=True)
    sub = lax.broadcasted_iota(jnp.int32, (128, 256), 0)
    mem, wrow = [], []
    for e in range(2):
        hit = routes_ref[...] == ep * 2 + e
        mem.append(jnp.sum(jnp.where(hit, 1.0, 0.0), axis=0, keepdims=True))
        wrow.append(jnp.sum(jnp.where(hit, rw, 0.0), axis=0, keepdims=True))
    memb = jnp.where(sub < 64, mem[0], mem[1])
    tri = jnp.where(
        lax.broadcasted_iota(jnp.int32, (256, 256), 0) < lax.broadcasted_iota(jnp.int32, (256, 256), 1), 1.0, 0.0
    ).astype(BF)
    rank = mm(memb.astype(BF), tri)
    slot = jnp.where(sub < 64, sub, sub - 64).astype(F32)
    chosen = jnp.where(rank == slot, memb, 0.0)
    psel[...] = chosen.astype(BF)
    spread_t = chosen.T
    weight_t = (chosen * jnp.where(sub < 64, wrow[0], wrow[1])).T
    lane = lax.broadcasted_iota(jnp.int32, (256, 128), 1)
    for e in range(2):
        inside = (lane < 64) if e == 0 else (lane >= 64)
        ptb[e] = jnp.where(inside, spread_t, 0.0).astype(BF)
        wcol[e] = jnp.broadcast_to(jnp.sum(jnp.where(inside, weight_t, 0.0), axis=1, keepdims=True), (256, 128))

    attended.relay()
    for d in near:
        attended.pass_on(d)

    weights[0].wait()
    weights[1].wait()

    def project(cc, half):
        total = jnp.zeros((256, 256), F32)
        for g in range(8):
            lhs = attg[cc, :, pl.ds(16 * g, 16), :].reshape(256, 128)
            total = total + mm(lhs, owb[g])
        total = total.reshape(16, 16, 256)
        total = total[:, :8, :128] + total[:, 8:, 128:]
        pb[x, cc] = total.reshape(128, 128).astype(BF)
        for d in near:
            remote(pb.at[x, cc], pb.at[x, cc], sb.at[0], rb.at[2 * d + half], peer(d, 0, 0)).start()

    project(c, 0)
    for d2 in (0,) + near:
        attended.arrived(d2)
        row = (a1 + 4 - d2) % 4
        total = jnp.zeros((64, 256), F32)
        for g in range(8):
            total = total + mm(attg[1 - c, pl.ds(4 * row, 4), pl.ds(16 * g, 16), :].reshape(64, 128), owb[g])
        total = total.reshape(4, 16, 256)
        total = total[:, :8, :128] + total[:, 8:, 128:]
        pb[x, 1 - c, pl.ds(pl.multiple_of(32 * row, 32), 32), :] = total.reshape(32, 128).astype(BF)
    for d in near:
        remote(pb.at[x, 1 - c], pb.at[x, 1 - c], sb.at[0], rb.at[2 * d + 1], peer(d, 0, 0)).start()
    attended.finish()
    weights[2].wait()
    for half, cc in ((0, c), (1, 1 - c)):
        for d in near:
            got(pb.at[(x + 4 - d) % 4, cc], rb.at[2 * d + half])
    for cc in range(2):
        total = pb[0, cc].astype(F32)
        for j in range(1, 4):
            total = total + pb[j, cc].astype(F32)
        total = total.reshape(16, 8, 128)
        for at in range(16):
            nat[at if cc == 0 else at % 4 * 4 + at // 4, cc] = total[at]
    hid[c, here] = (resb[...].astype(F32) + nat[...].reshape(256, 128)).astype(BF)

    hidden = Gather(hid, sc, rc, scs, rcs)
    hidden.start()
    sent(pb.at[pl.ds(0, 3)], sb.at[0])
    block[...] = hid[c, here].astype(F32).T
    hidden.relay()
    for w in weights[3:]:
        w.wait()

    def products(d2, cc, first):
        row = ((a2 if cc is c else a1) + 4 - d2) % 4
        at = [(4 * row + k) * (1 - cc) + (4 * k + row) * cc for k in range(4)]
        picked = mm(psel[...], jnp.concatenate([hid[cc, 4 * row + k] for k in range(4)], axis=1))
        squares = picked * picked
        gain = jnp.concatenate([gain_ref[pl.ds(2 * b + cc, 1), :] for b in at], axis=1)
        squares = squares[:, :128] + squares[:, 128:256] + squares[:, 256:384] + squares[:, 384:]
        lhs = (picked * gain).astype(BF)
        cols = [pl.ds(pl.multiple_of((2 * b + cc) * 128, 128), 128) for b in at]
        for e in range(2):
            rhs = jnp.concatenate([gu[e, col, :] for col in cols], axis=0)
            part = mm(lhs[64 * e : 64 * e + 64], rhs)
            acc[e] = part if first else acc[e] + part
        sq[...] = squares if first else sq[...] + squares

    products(0, c, True)
    waiting = 0
    for d2 in near:
        hidden.pass_on(d2)
        hidden.arrived(waiting)
        products(waiting, 1 - c, False)
        products(d2, c, False)
        waiting = d2
    hidden.arrived(waiting)
    products(waiting, 1 - c, False)
    rs = lax.rsqrt(jnp.sum(sq[...], axis=1, keepdims=True) / 4096 + EPSILON)
    halves = []
    for e in range(2):
        re = rs[64 * e : 64 * e + 64]
        gate = acc[e, :, pl.ds(0, 384)] * re
        up = acc[e, :, pl.ds(384, 384)] * re
        halves.append((gate / (1.0 + jnp.exp(-gate)) * up).astype(BF))
    act = jnp.concatenate(halves, axis=0)
    for e in range(2):
        spread = mm(ptb[e], act)
        aact[:, pl.ds(384 * e, 384)] = (spread * wcol[e][:, :1]).astype(BF)

    def turn(i):
        return jnp.where(i == 0, 2, jnp.where(i == 1, 1, jnp.where(i == 2, 3, 0)))

    def dest(n, cc):
        d1 = jnp.where(n < 12, turn(n % 3), 0)
        d2 = turn(jnp.where(n < 12, n // 3, n - 12))
        dy = d1 * (1 - cc) + d2 * cc
        dz = d2 * (1 - cc) + d1 * cc
        return d1, d2, (y + dy) % 4 * 4 + (z + dz) % 4

    def down(n):
        mine_col = pl.multiple_of((2 * dest(n, c)[2] + c) * 128, 128)
        sib_col = pl.multiple_of((2 * dest(n, 1 - c)[2] + 1 - c) * 128, 128)
        rhs = jnp.concatenate([dn[:, pl.ds(sib_col, 128)], dn[:, pl.ds(mine_col, 128)]], axis=1)
        both = mm(aact[...], rhs)
        psib[n] = both[:, :128].astype(BF)
        remote(psib.at[n], srec.at[n], sds.at[0], rds.at[n], sib).start()
        pown[n] = both[:, 128:]

    def join(n):
        got(srec.at[n], rds.at[n])
        return pown[n] + srec[n].astype(F32)

    def forward(n):
        d1, d2, _ = dest(n, c)
        qbuf[n] = join(n).astype(BF)
        remote(qbuf.at[n], r1.at[d2, n % 3], sd1.at[0], rd1.at[d2], peer(0, d1 * (1 - c), d1 * c)).start()

    for n in range(LAG):
        down(n)

    def step(n, _):
        down(n)
        forward(n - LAG)
        return 0

    lax.fori_loop(LAG, 12 + LAG, step, 0)
    for n in range(12 + LAG, 16):
        down(n)
    hidden.finish()

    def slab(j):
        return pl.ds(pl.multiple_of(32 * (j % 4), 32), 32)

    for i2, d2 in enumerate((2, 1, 3, 0)):
        total = join(12 + i2)
        got(r1.at[d2], rd1.at[d2])
        for i1 in range(3):
            total = total + r1[d2, i1].astype(F32)
        turned = total.T
        tb[d2] = turned.astype(BF)
        if d2 == 0:
            last[...] = block[slab(x), :] + jnp.where(x == 0, turned[:32], jnp.where(x == 1, turned[32:64], jnp.where(x == 2, turned[64:96], turned[96:])))
        for dx in (2, 1, 3, 0):
            if d2 or dx:
                dev = peer(dx, d2 * c, d2 * (1 - c))
                remote(tb.at[d2, slab(x + dx)], r2.at[4 * d2 + dx], sd2.at[0], rd2.at[0], dev).start()
    sent(psib, sds.at[0])
    sent(qbuf, sd1.at[0])
    got(r2.at[pl.ds(1, 15)], rd2.at[0])
    total = last[...]
    for k in range(1, 16):
        total = total + r2[k].astype(F32)
    out_ref[...] = total.astype(BF)
    sent(r2.at[pl.ds(1, 15)], sd2.at[0])


def per_device(
    queries, key_cache, stored_value_cache, new_key, incoming_value, lengths, policy, retained_blocks,
    out_weight, residual, norm_gain, routes, router_logits, gate_weight, up_weight, down_weight,
):
    vm = pl.BlockSpec(memory_space=pltpu.VMEM)
    hb = pl.BlockSpec(memory_space=pl.ANY)
    dma = pltpu.SemaphoreType.DMA
    scratch = [
        pltpu.SMEM((8,), jnp.int32),
        pltpu.SMEM((8,), jnp.int32),
        pltpu.SMEM((4, 8), jnp.int32),
        pltpu.VMEM((8, 16, 128), BF),
        pltpu.VMEM((8, 128), BF),
        pltpu.VMEM((8, 128), BF),
        pltpu.VMEM((8, 256), jnp.int32),
        pltpu.VMEM((8, 256), F32),
        pltpu.VMEM((32, 128), F32),
        pltpu.VMEM((8, 1024, 128), BF),
        pltpu.VMEM((8, 1024, 128), BF),
        pltpu.VMEM((8, 16, 1024), BF),
        pltpu.VMEM((8, 16, 128), F32),
        pltpu.VMEM((8, 16, 128), BF),
        pltpu.VMEM((16, 8, 128), F32),
        pltpu.VMEM((2, 16, 128, 128), BF),
        pltpu.VMEM((8, 128, 256), BF),
        pltpu.VMEM((4, 2, 128, 128), BF),
        pltpu.VMEM((16, 2, 8, 128), F32),
        pltpu.VMEM((256, 128), BF),
        pltpu.VMEM((2, 16, 256, 128), BF),
        pltpu.VMEM((128, 128), F32),
        pltpu.VMEM((2, 4096, 768), BF),
        pltpu.VMEM((768, 4096), BF),
        pltpu.VMEM((2, 256, 128), BF),
        pltpu.VMEM((128, 256), BF),
        pltpu.VMEM((2, 256, 128), F32),
        pltpu.VMEM((2, 64, 768), F32),
        pltpu.VMEM((256, 768), BF),
        pltpu.VMEM((16, 256, 128), BF),
        pltpu.VMEM((16, 256, 128), F32),
        pltpu.VMEM((16, 256, 128), BF),
        pltpu.VMEM((12, 256, 128), BF),
        pltpu.VMEM((4, 3, 256, 128), BF),
        pltpu.VMEM((4, 128, 256), BF),
        pltpu.VMEM((32, 256), F32),
        pltpu.VMEM((128, 256), F32),
        pltpu.VMEM((16, 32, 256), BF),
        dma((9,)), dma((4,)), dma((4,)), dma((8,)),
        dma((1,)), dma((12,)), dma((1,)), dma((4,)),
        dma((1,)), dma((8,)),
        dma((1,)), dma((12,)), dma((1,)), dma((4,)),
        dma((1,)), dma((16,)), dma((1,)), dma((4,)),
        dma((1,)), dma((1,)),
    ]
    return pl.pallas_call(
        kernel,
        out_shape=jax.ShapeDtypeStruct((32, 256), BF),
        in_specs=[hb] * 16,
        out_specs=vm,
        scratch_shapes=scratch,
        name="decode_step",
        cost_estimate=pl.CostEstimate(flops=3_000_000_000, bytes_accessed=26_000_000, transcendentals=200_000),
        compiler_params=pltpu.CompilerParams(
            collective_id=0, has_side_effects=True, vmem_limit_bytes=56 * 2**20
        ),
    )(
        lengths, policy.reshape(8), retained_blocks.transpose(1, 2, 0).reshape(4, 8),
        queries, new_key.reshape(8, 128), incoming_value.reshape(8, 128),
        routes.T, router_logits.T, norm_gain.reshape(32, 128),
        key_cache.reshape(8, 1024, 128), stored_value_cache.reshape(8, 1024, 128),
        out_weight.reshape(32, 2, 128, 128), residual,
        gate_weight, up_weight, down_weight.reshape(768, 4096),
    ).T


def solution(mesh):
    return jax.shard_map(
        per_device,
        mesh=mesh,
        in_specs=(
            P("ep", "tp", None),
            P("ep", "tp", None, None),
            P("ep", "tp", None, None),
            P("ep", "tp", None),
            P("ep", "tp", None),
            P("ep"),
            P("ep", "tp"),
            P("ep", "tp", None),
            P(None, "ep"),
            P(None, "ep"),
            P(),
            P(),
            P(),
            P("ep", None, "tp"),
            P("ep", None, "tp"),
            P("ep", "tp", None),
        ),
        out_specs=P(None, ("ep", "tp")),
        check_vma=False,
    )
```
